32 devices in a mesh: ev: 2 (over x), sp: 16 (over z, y, core).
Axes of the slice: x: 2, y: 2, z: 4, core: 2. Of those that a mesh axis runs over, the one named last changes fastest.
Arguments:
- partial_kernels: float32 [2, 32, 32, 128], P('ev', None, 'sp'), may hold values from -6 to 6
- block_ids: int32 [2, 32], P('ev', 'sp'), may hold values from 0 to 63, as said below
- radial_smoother: float32 [128, 128], replicated, may hold values from -0.5 to 2
- shell_level: int32 [128], P('sp'), may hold values from 1 to 4
- lateral_scale: float32 [128, 256], replicated, may hold values from 0.5 to 1
Outputs:
- smoothed_kernel: float32 [128, 128, 256], P('sp', None, 'ev')
The draws below stay inside these ranges and needn't reach their ends.
Inputs may be any that keep to these rules, and one draw needn't show every extreme that they name: `block_ids`: each index of ev and sp holds 2 distinct ids; an id's owner is id // 32; one holder gives at most 2 ids to one owner, and in every stripe some owner receives 2 ids from every group.
All inputs are finite; a program needn't handle non-finite values.
Results may differ from the reference program's by a relative error of at most 0.000073.
Values sent between devices are 32-bit elements; how exact they have to be, the bound alone decides.
A program may use at most 64 MiB of HBM per device.

```python
import jax
import jax.numpy as jnp
from jax import lax

NR = 128
RB = 32
BY = 128
BPT = 8
PASSES = 4
LIST = 2
NSEG = 4
LX = 128
LY = 256
N_EV = 2
N_SP = 16


def draw_block_ids(key, part):
    subkeys = jax.random.split(key, 6)
    per_owner = BPT * NSEG
    favored = jax.random.randint(subkeys[0], (1, N_SP, 1), 0, N_EV)
    scores = jax.random.randint(subkeys[1], (N_EV, N_SP, N_EV - 1), 0, 1 << 20) * N_EV + jnp.arange(N_EV - 1)
    others = jnp.argsort(scores, axis=-1).astype(jnp.int32) + 1
    owner_order = (favored + jnp.concatenate([jnp.zeros((N_EV, N_SP, 1), jnp.int32), others], axis=-1)) % N_EV
    leading = owner_order[..., 0::2]
    trailing = owner_order[..., 1::2]
    doubled = jax.random.randint(subkeys[2], (N_EV, N_SP, N_EV // 2), 0, 2)
    doubled = doubled.at[..., 0].set(1)
    partner = jnp.where(doubled == 1, leading, trailing)
    spot_first = jax.random.randint(subkeys[3], (N_EV, N_SP, N_EV // 2), 0, per_owner)
    spot_second = (spot_first + 1 + jax.random.randint(subkeys[4], (N_EV, N_SP, N_EV // 2), 0, per_owner - 1)) % per_owner
    entry_owner = jnp.stack([leading, partner], axis=-1).reshape(N_EV, N_SP, N_EV)
    entry_spot = jnp.stack([spot_first, spot_second], axis=-1).reshape(N_EV, N_SP, N_EV)
    block_list = entry_owner * per_owner + entry_spot
    shuffle_scores = jax.random.randint(subkeys[5], (N_EV, N_SP, N_EV), 0, 1 << 20) * N_EV + jnp.arange(N_EV)
    shuffled_order = jnp.argsort(shuffle_scores, axis=-1)
    block_list = jnp.take_along_axis(block_list, shuffled_order, axis=-1)
    return block_list.reshape(N_EV, N_SP * N_EV).astype(jnp.int32)


def draw_radial_smoother(key, part):
    key_diag, key_off = jax.random.split(key)
    row_index = jnp.arange(NR)[:, None]
    col_index = jnp.arange(NR)[None, :]
    distance = jnp.abs(row_index - col_index).astype(jnp.float32)
    offdiag = jax.random.uniform(key_off, (NR, NR), jnp.float32, minval=-1.0, maxval=1.0)
    diag_part = jax.random.uniform(key_diag, (NR,), jnp.float32, minval=0.8, maxval=1.4)
    matrix = 0.15 * jnp.exp(-distance / 6.0) * offdiag + jnp.where(distance == 0.0, diag_part[:, None], 0.0)
    return matrix.astype(jnp.float32)


def place_ends(array, own_key, low, largest):
    spot = [jax.random.randint(jax.random.fold_in(own_key, axis), (), 0, length) for axis, length in enumerate(array.shape)]
    main_axis = array.shape.index(max(array.shape))
    beside = spot[:main_axis] + [(spot[main_axis] + 1) % array.shape[main_axis]] + spot[main_axis + 1:]
    return array.at[tuple(spot)].set(low).at[tuple(beside)].set(largest)


def levels(stream_key, shape, cuts, smallest, largest):
    def one(axis_at, parts):
        draws = jax.random.uniform(jax.random.fold_in(jax.random.fold_in(stream_key, 6), axis_at), (parts,), jnp.float32, smallest / len(cuts), largest / len(cuts))
        return jnp.repeat(jnp.exp(draws), shape[axis_at] // parts).reshape((-1,) + (1,) * (len(shape) - axis_at - 1))

    gain = one(*cuts[0])
    for cut in cuts[1:]:
        gain = gain * one(*cut)
    return gain


def centred(own_key, extent, width, limit, cuts=(), kind=jnp.bfloat16):
    entries = jax.random.normal(own_key, extent, jnp.float32) * width
    if len(cuts) > 0:
        entries = levels(own_key, extent, cuts, -0.22, 0.18) * entries
    return jnp.clip(entries, min=-limit, max=limit).astype(kind)


def setup_inputs(seed: int = 0) -> dict:
    key_list = jax.random.split(jax.random.key(seed), 6)
    return {
        "partial_kernels": centred(key_list[0], (N_EV, RB, N_SP * LIST, BY), 1.0, 6.0, ((0, 2), (2, 16)), jnp.float32),
        "block_ids": draw_block_ids(jax.random.fold_in(key_list[5], 71), 0),
        "radial_smoother": draw_radial_smoother(jax.random.fold_in(key_list[5], 71), 0),
        "shell_level": place_ends(jax.random.randint(key_list[3], (NR,), 1, 5), jax.random.fold_in(key_list[3], 1), 1, 4).astype(jnp.int32),
        "lateral_scale": jnp.clip(jax.random.uniform(key_list[4], (LX, LY), jnp.float32, 0.5, 1.0), 0.5, 1.0),
    }


diffusion_rate = 0.0615


def reference(partial_kernels, block_ids, radial_smoother, shell_level, lateral_scale):
    per_owner = BPT * NSEG
    stripe = (jnp.arange(N_SP * LIST, dtype=jnp.int32) // LIST)[None, :]
    owners = block_ids // per_owner
    within = block_ids % per_owner
    row_in = within // NSEG
    seg_of = within % NSEG
    x_place = (stripe * BPT + row_in).reshape(-1).astype(jnp.int32)
    y_place = owners.reshape(-1).astype(jnp.int32)
    seg_place = seg_of.reshape(-1).astype(jnp.int32)
    blocks = jnp.transpose(partial_kernels, (0, 2, 1, 3)).reshape(N_EV * N_SP * LIST, RB, BY)
    grid_sum = jnp.zeros((NSEG, LX, N_EV, RB, BY), jnp.float32)
    grid_sum = grid_sum.at[seg_place, x_place, y_place].add(blocks)
    kernel = jnp.transpose(grid_sum, (0, 3, 1, 2, 4)).reshape(NR, LX * LY)
    smoothed = jnp.dot(radial_smoother, kernel, precision=lax.Precision.HIGHEST).reshape(NR, LX, LY)
    coefficient = diffusion_rate * shell_level.astype(jnp.float32)[:, None, None] * lateral_scale[None]
    kernel_field = smoothed
    for repeat in range(PASSES):
        padded = jnp.pad(kernel_field, ((0, 0), (1, 1), (1, 1)))
        beside = padded[:, 2:, 1:-1] + padded[:, :-2, 1:-1] + padded[:, 1:-1, 2:] + padded[:, 1:-1, :-2]
        kernel_field = kernel_field + coefficient * (beside - 4.0 * kernel_field)
    return kernel_field
```

```python
import functools

import jax
import jax.numpy as jnp
from jax import lax
from jax.experimental import pallas as pl
from jax.experimental.pallas import tpu as pltpu
from jax.sharding import PartitionSpec as P

BPT = 8
PASSES = 4
NSEG = 4
MESH = pl.DeviceIdType.MESH

diffusion_rate = 0.0615


def kernel(
    n_ev, n_sp, ids, levels, blocks, smoother, scale, out,
    outgoing, label_out, arrived, labels, here, there, beside_here, beside_there, coef, beside_coef,
    send_sem, recv_sem, label_send_sem, label_recv_sem,
):
    count = n_ev * n_sp
    ev, sp = lax.axis_index("ev"), lax.axis_index("sp")
    me = ev * n_sp + sp
    rows, shells, width = coef.shape
    listed, depth = blocks.shape[2], blocks.shape[1]

    def device(step):
        target = lax.rem(me + step, count)
        return target // n_sp, lax.rem(target, n_sp)

    barrier = pltpu.get_barrier_semaphore()

    def greet(step, carry):
        pl.semaphore_signal(barrier, inc=1, device_id=device(step), device_id_type=MESH)
        return carry

    lax.fori_loop(1, count, greet, 0)

    for j in range(listed):
        block_id = ids[0, j]
        label_out[j : j + 1, :] = jnp.full((1, width), block_id // NSEG, jnp.int32)
        segment = lax.rem(block_id, NSEG)
        block = blocks[0, :, j, :]
        column = jnp.concatenate(
            [block * (segment == q).astype(jnp.float32) for q in range(NSEG)], axis=0
        )
        smooth = jnp.dot(
            smoother[...], column, precision=lax.Precision.HIGHEST, preferred_element_type=jnp.float32
        )
        for m in range(n_sp):
            outgoing[m, j * shells : (j + 1) * shells, :] = smooth[m * shells : (m + 1) * shells, :]

    pl.semaphore_wait(barrier, count - 1)

    def label_copy(step):
        return pltpu.make_async_remote_copy(
            src_ref=label_out, dst_ref=labels.at[me], send_sem=label_send_sem,
            recv_sem=label_recv_sem, device_id=device(step), device_id_type=MESH,
        )

    def copy(step):
        return pltpu.make_async_remote_copy(
            src_ref=outgoing.at[device(step)[1]], dst_ref=arrived.at[me], send_sem=send_sem,
            recv_sem=recv_sem, device_id=device(step), device_id_type=MESH,
        )

    def send(step, carry):
        copy(step).start()
        label_copy(step).start()
        return carry

    lax.fori_loop(1, count, send, 0)

    arrived[me] = outgoing[sp]
    labels[me] = label_out[...]

    shell_of = lax.broadcasted_iota(jnp.int32, (shells, width), 0)
    level = jnp.zeros((shells, width), jnp.float32)
    for r in range(shells):
        level = jnp.where(shell_of == r, levels[r].astype(jnp.float32), level)
    level = diffusion_rate * level
    lane = lax.broadcasted_iota(jnp.int32, (1, width), 1)
    right_half = lane < width // 2
    after = jnp.minimum(ev + 1, n_ev - 1)
    before = jnp.maximum(ev - 1, 0)
    inside = jnp.where(right_half, (ev + 1 < n_ev).astype(jnp.float32), (ev > 0).astype(jnp.float32))

    def tile(start, which):
        return scale[pl.ds(start, BPT), pl.ds(pl.multiple_of(which * width, width), width)]

    def coefficients(stripe, carry):
        start = pl.multiple_of(stripe * BPT, BPT)
        main = tile(start, ev)
        sides = jnp.where(right_half, tile(start, after), tile(start, before)) * inside
        coef[pl.ds(start, BPT)] = level[None] * main[:, None, :]
        beside_coef[pl.ds(start, BPT)] = level[None] * sides[:, None, :]
        return carry

    lax.fori_loop(0, n_sp, coefficients, 0)
    blank = jnp.zeros((1, shells, width), jnp.float32)
    for field in (here, there, beside_here, beside_there):
        field[0:1] = blank
        field[rows + 1 : rows + 2] = blank

    def all_of(buffer, one, two):
        whole = buffer.at[pl.ds(0, count - 1)]
        return pltpu.make_async_remote_copy(
            src_ref=whole, dst_ref=whole, send_sem=one, recv_sem=two,
            device_id=device(1), device_id_type=MESH,
        )

    all_of(labels, label_send_sem, label_recv_sem).wait_recv()
    all_of(arrived, send_sem, recv_sem).wait_recv()

    side_tile = jnp.where(right_half, ev + 1, ev - 1) * BPT

    def place(stripe, carry):
        main = [jnp.zeros((shells, width), jnp.float32) for _ in range(BPT)]
        sides = list(main)
        for g in range(n_ev):
            source = g * n_sp + stripe
            for j in range(listed):
                block = arrived[source, j * shells : (j + 1) * shells, :]
                label = jnp.broadcast_to(labels[source, j : j + 1, :], (shells, width))
                in_main = label - ev * BPT
                in_sides = label - side_tile
                for k in range(BPT):
                    main[k] = main[k] + jnp.where(in_main == k, block, 0.0)
                    sides[k] = sides[k] + jnp.where(in_sides == k, block, 0.0)
        for k in range(BPT):
            here[stripe * BPT + 1 + k] = main[k]
            beside_here[stripe * BPT + 1 + k] = sides[k]
        return carry

    lax.fori_loop(0, n_sp, place, 0)

    at_end = (lane == width - 1)[None]
    at_start = (lane == 0)[None]

    def diffuse(field, side_field, new_field, new_side, last):
        def chunk(stripe, carry):
            start = stripe * BPT
            main = field[pl.ds(start + 1, BPT)]
            sides = side_field[pl.ds(start + 1, BPT)]
            main_up, sides_up = pltpu.roll(main, width - 1, 2), pltpu.roll(sides, width - 1, 2)
            main_down, sides_down = pltpu.roll(main, 1, 2), pltpu.roll(sides, 1, 2)
            around = (
                field[pl.ds(start + 2, BPT)] + field[pl.ds(start, BPT)]
                + jnp.where(at_end, sides_up, main_up)
                + jnp.where(at_start, sides_down, main_down)
            )
            new = main + coef[pl.ds(start, BPT)] * (around - 4.0 * main)
            if last:
                new_field[pl.ds(start, BPT)] = new
                return carry
            new_field[pl.ds(start + 1, BPT)] = new
            around = (
                side_field[pl.ds(start + 2, BPT)] + side_field[pl.ds(start, BPT)]
                + jnp.where(at_end, main_up, sides_up)
                + jnp.where(at_start, main_down, sides_down)
            )
            new_side[pl.ds(start + 1, BPT)] = sides + beside_coef[pl.ds(start, BPT)] * (around - 4.0 * sides)
            return carry

        lax.fori_loop(0, n_sp, chunk, 0)

    now, later = (here, beside_here), (there, beside_there)
    for repeat in range(PASSES):
        last = repeat == PASSES - 1
        diffuse(*now, *((out, None) if last else later), last)
        now, later = later, now

    all_of(labels, label_send_sem, label_recv_sem).wait_send()
    all_of(arrived, send_sem, recv_sem).wait_send()


def solution(mesh):
    n_ev, n_sp = mesh.shape["ev"], mesh.shape["sp"]
    count = n_ev * n_sp

    def per_device(partial_kernels, block_ids, radial_smoother, shell_level, lateral_scale):
        listed, width = partial_kernels.shape[2:]
        shells = shell_level.shape[0]
        rows = lateral_scale.shape[0]
        field = pltpu.VMEM((rows + 2, shells, width), jnp.float32)
        inner = pltpu.VMEM((rows, shells, width), jnp.float32)
        smem = pl.BlockSpec(memory_space=pltpu.SMEM)
        vmem = pl.BlockSpec(memory_space=pltpu.VMEM)
        out = pl.pallas_call(
            functools.partial(kernel, n_ev, n_sp),
            out_shape=jax.ShapeDtypeStruct((rows, shells, width), jnp.float32),
            in_specs=[smem, smem, vmem, vmem, vmem],
            out_specs=vmem,
            scratch_shapes=[
                pltpu.VMEM((n_sp, listed * shells, width), jnp.float32),
                pltpu.VMEM((listed, width), jnp.int32),
                pltpu.VMEM((count, listed * shells, width), jnp.float32),
                pltpu.VMEM((count, listed, width), jnp.int32),
                field, field, field, field, inner, inner,
            ]
            + [pltpu.SemaphoreType.DMA] * 4,
            compiler_params=pltpu.CompilerParams(
                collective_id=0, has_side_effects=True, vmem_limit_bytes=40 * 1024 * 1024
            ),
        )(block_ids, shell_level, partial_kernels, radial_smoother, lateral_scale)
        return jnp.transpose(out, (1, 0, 2))

    placed = (P("ev", None, "sp", None), P("ev", "sp"), P(), P("sp"), P())
    return jax.shard_map(
        per_device, mesh=mesh, in_specs=placed, out_specs=P("sp", None, "ev"), check_vma=False
    )
```

```python
import functools

import jax
import jax.numpy as jnp
from jax import lax
from jax.experimental import pallas as pl
from jax.experimental.pallas import tpu as pltpu
from jax.sharding import PartitionSpec as P

BPT = 8
PASSES = 4
NSEG = 4
MESH = pl.DeviceIdType.MESH

diffusion_rate = 0.0615


def kernel(
    n_ev, n_sp, ids_in, levels_in, blocks_in, smoother_in, scale_in, out,
    ids, levels, blocks, smoother, scale,
    outgoing, label_out, arrived, labels, here, there, beside_here, beside_there, coef, beside_coef,
    send_sem, recv_sem, label_send_sem, label_recv_sem, load_sem, store_sem,
):
    count = n_ev * n_sp
    ev, sp = lax.axis_index("ev"), lax.axis_index("sp")
    me = ev * n_sp + sp
    rows, shells, width = coef.shape
    listed, depth = blocks.shape[2], blocks.shape[1]

    def device(step):
        target = lax.rem(me + step, count)
        return target // n_sp, lax.rem(target, n_sp)

    loads = [
        pltpu.make_async_copy(given, held, load_sem.at[i])
        for i, (given, held) in enumerate(
            [(ids_in, ids), (blocks_in, blocks), (smoother_in, smoother), (levels_in, levels), (scale_in, scale)]
        )
    ]
    for load in loads:
        load.start()

    barrier = pltpu.get_barrier_semaphore()

    def greet(step, carry):
        pl.semaphore_signal(barrier, inc=1, device_id=device(step), device_id_type=MESH)
        return carry

    lax.fori_loop(1, count, greet, 0)

    for load in loads[:3]:
        load.wait()

    for j in range(listed):
        block_id = ids[0, j]
        label_out[j : j + 1, :] = jnp.full((1, width), block_id // NSEG, jnp.int32)
        segment = lax.rem(block_id, NSEG)
        block = blocks[0, :, j, :]
        column = jnp.concatenate(
            [block * (segment == q).astype(jnp.float32) for q in range(NSEG)], axis=0
        )
        smooth = jnp.dot(
            smoother[...], column, precision=lax.Precision.HIGHEST, preferred_element_type=jnp.float32
        )
        for m in range(n_sp):
            outgoing[m, j * shells : (j + 1) * shells, :] = smooth[m * shells : (m + 1) * shells, :]

    pl.semaphore_wait(barrier, count - 1)

    def label_copy(step):
        return pltpu.make_async_remote_copy(
            src_ref=label_out, dst_ref=labels.at[me], send_sem=label_send_sem,
            recv_sem=label_recv_sem, device_id=device(step), device_id_type=MESH,
        )

    def copy(step):
        return pltpu.make_async_remote_copy(
            src_ref=outgoing.at[device(step)[1]], dst_ref=arrived.at[me], send_sem=send_sem,
            recv_sem=recv_sem, device_id=device(step), device_id_type=MESH,
        )

    def send(step, carry):
        copy(step).start()
        label_copy(step).start()
        return carry

    lax.fori_loop(1, count, send, 0)

    arrived[me] = outgoing[sp]
    labels[me] = label_out[...]

    for load in loads[3:]:
        load.wait()

    shell_of = lax.broadcasted_iota(jnp.int32, (shells, width), 0)
    level = jnp.zeros((shells, width), jnp.float32)
    for r in range(shells):
        level = jnp.where(shell_of == r, levels[r].astype(jnp.float32), level)
    level = diffusion_rate * level
    lane = lax.broadcasted_iota(jnp.int32, (1, width), 1)
    right_half = lane < width // 2
    after = jnp.minimum(ev + 1, n_ev - 1)
    before = jnp.maximum(ev - 1, 0)
    inside = jnp.where(right_half, (ev + 1 < n_ev).astype(jnp.float32), (ev > 0).astype(jnp.float32))

    def tile(start, which):
        return scale[pl.ds(start, BPT), pl.ds(pl.multiple_of(which * width, width), width)]

    def coefficients(stripe, carry):
        start = pl.multiple_of(stripe * BPT, BPT)
        main = tile(start, ev)
        sides = jnp.where(right_half, tile(start, after), tile(start, before)) * inside
        coef[pl.ds(start, BPT)] = level[None] * main[:, None, :]
        beside_coef[pl.ds(start, BPT)] = level[None] * sides[:, None, :]
        return carry

    lax.fori_loop(0, n_sp, coefficients, 0)
    blank = jnp.zeros((1, shells, width), jnp.float32)
    for field in (here, there, beside_here, beside_there):
        field[0:1] = blank
        field[rows + 1 : rows + 2] = blank

    def all_of(buffer, one, two):
        whole = buffer.at[pl.ds(0, count - 1)]
        return pltpu.make_async_remote_copy(
            src_ref=whole, dst_ref=whole, send_sem=one, recv_sem=two,
            device_id=device(1), device_id_type=MESH,
        )

    all_of(labels, label_send_sem, label_recv_sem).wait_recv()
    all_of(arrived, send_sem, recv_sem).wait_recv()

    side_tile = jnp.where(right_half, ev + 1, ev - 1) * BPT

    def place(stripe, carry):
        main = [jnp.zeros((shells, width), jnp.float32) for _ in range(BPT)]
        sides = list(main)
        for g in range(n_ev):
            source = g * n_sp + stripe
            for j in range(listed):
                block = arrived[source, j * shells : (j + 1) * shells, :]
                label = jnp.broadcast_to(labels[source, j : j + 1, :], (shells, width))
                in_main = label - ev * BPT
                in_sides = label - side_tile
                for k in range(BPT):
                    main[k] = main[k] + jnp.where(in_main == k, block, 0.0)
                    sides[k] = sides[k] + jnp.where(in_sides == k, block, 0.0)
        for k in range(BPT):
            here[stripe * BPT + 1 + k] = main[k]
            beside_here[stripe * BPT + 1 + k] = sides[k]
        return carry

    lax.fori_loop(0, n_sp, place, 0, unroll=2)

    at_end = (lane == width - 1)[None]
    at_start = (lane == 0)[None]

    def diffuse(field, side_field, new_field, new_side, last):
        def chunk(stripe, carry):
            start = stripe * BPT
            main = field[pl.ds(start + 1, BPT)]
            sides = side_field[pl.ds(start + 1, BPT)]
            main_up, sides_up = pltpu.roll(main, width - 1, 2), pltpu.roll(sides, width - 1, 2)
            main_down, sides_down = pltpu.roll(main, 1, 2), pltpu.roll(sides, 1, 2)
            around = (
                field[pl.ds(start + 2, BPT)] + field[pl.ds(start, BPT)]
                + jnp.where(at_end, sides_up, main_up)
                + jnp.where(at_start, sides_down, main_down)
            )
            new = main + coef[pl.ds(start, BPT)] * (around - 4.0 * main)
            new_field[pl.ds(start + 1, BPT)] = new
            if last:
                pltpu.make_async_copy(
                    new_field.at[pl.ds(start + 1, BPT)], out.at[pl.ds(start, BPT)], store_sem
                ).start()
                return carry
            around = (
                side_field[pl.ds(start + 2, BPT)] + side_field[pl.ds(start, BPT)]
                + jnp.where(at_end, main_up, sides_up)
                + jnp.where(at_start, main_down, sides_down)
            )
            new_side[pl.ds(start + 1, BPT)] = sides + beside_coef[pl.ds(start, BPT)] * (around - 4.0 * sides)
            return carry

        lax.fori_loop(0, n_sp, chunk, 0, unroll=2)

    now, later = (here, beside_here), (there, beside_there)
    for repeat in range(PASSES):
        last = repeat == PASSES - 1
        diffuse(*now, *later, last)
        now, later = later, now

    all_of(labels, label_send_sem, label_recv_sem).wait_send()
    all_of(arrived, send_sem, recv_sem).wait_send()
    pltpu.make_async_copy(now[0].at[pl.ds(1, rows)], out, store_sem).wait()


def solution(mesh):
    n_ev, n_sp = mesh.shape["ev"], mesh.shape["sp"]
    count = n_ev * n_sp

    def per_device(partial_kernels, block_ids, radial_smoother, shell_level, lateral_scale):
        listed, width = partial_kernels.shape[2:]
        shells = shell_level.shape[0]
        rows = lateral_scale.shape[0]
        field = pltpu.VMEM((rows + 2, shells, width), jnp.float32)
        inner = pltpu.VMEM((rows, shells, width), jnp.float32)
        out = pl.pallas_call(
            functools.partial(kernel, n_ev, n_sp),
            out_shape=jax.ShapeDtypeStruct((rows, shells, width), jnp.float32),
            in_specs=[pl.BlockSpec(memory_space=pltpu.HBM)] * 5,
            out_specs=pl.BlockSpec(memory_space=pltpu.HBM),
            scratch_shapes=[
                pltpu.SMEM(block_ids.shape, jnp.int32),
                pltpu.SMEM(shell_level.shape, jnp.int32),
                pltpu.VMEM(partial_kernels.shape, jnp.float32),
                pltpu.VMEM(radial_smoother.shape, jnp.float32),
                pltpu.VMEM(lateral_scale.shape, jnp.float32),
                pltpu.VMEM((n_sp, listed * shells, width), jnp.float32),
                pltpu.VMEM((listed, width), jnp.int32),
                pltpu.VMEM((count, listed * shells, width), jnp.float32),
                pltpu.VMEM((count, listed, width), jnp.int32),
                field, field, field, field, inner, inner,
            ]
            + [pltpu.SemaphoreType.DMA] * 4
            + [pltpu.SemaphoreType.DMA((5,)), pltpu.SemaphoreType.DMA],
            compiler_params=pltpu.CompilerParams(
                collective_id=0, has_side_effects=True, vmem_limit_bytes=63 * 1024 * 1024
            ),
        )(block_ids, shell_level, partial_kernels, radial_smoother, lateral_scale)
        return jnp.transpose(out, (1, 0, 2))

    placed = (P("ev", None, "sp", None), P("ev", "sp"), P(), P("sp"), P())
    return jax.shard_map(
        per_device, mesh=mesh, in_specs=placed, out_specs=P("sp", None, "ev"), check_vma=False
    )
```

```python
import functools

import jax
import jax.numpy as jnp
from jax import lax
from jax.experimental import pallas as pl
from jax.experimental.pallas import tpu as pltpu
from jax.sharding import PartitionSpec as P

BPT = 8
PASSES = 4
NSEG = 4
MESH = pl.DeviceIdType.MESH

diffusion_rate = 0.0615


def kernel(
    n_ev, n_sp, ids_in, levels_in, blocks_in, smoother_in, scale_in, out,
    ids, levels, blocks, smoother, scale,
    outgoing, label_out, arrived, labels, here, there, beside_here, beside_there, coef, beside_coef, final,
    load_sem, send_sem, recv_sem, label_send_sem, label_recv_sem,
    pass_send_sem, pass_recv_sem, label_pass_send_sem, label_pass_recv_sem, store_sem,
):
    ev, sp = lax.axis_index("ev"), lax.axis_index("sp")
    rows, shells, width = coef.shape
    listed = blocks.shape[2]
    groups = recv_sem.shape[0]
    size = n_sp // groups

    loads = [
        pltpu.make_async_copy(given, held, load_sem.at[i])
        for i, (given, held) in enumerate(
            [(ids_in, ids), (blocks_in, blocks), (smoother_in, smoother), (levels_in, levels), (scale_in, scale)]
        )
    ]
    for load in loads:
        load.start()

    def holder(step):
        return lax.rem(sp + step, n_sp)

    def peer(step):
        return lax.rem(ev + step, n_ev)

    barrier = pltpu.get_barrier_semaphore()

    def greet(step, carry):
        pl.semaphore_signal(barrier, inc=1, device_id=(ev, holder(step)), device_id_type=MESH)
        return carry

    lax.fori_loop(1, n_sp, greet, 0)
    for step in range(1, n_ev):
        pl.semaphore_signal(barrier, inc=1, device_id=(peer(step), sp), device_id_type=MESH)

    for load in loads[:3]:
        load.wait()
    columns = []
    for j in range(listed):
        block_id = ids[0, j]
        label_out[j : j + 1, :] = jnp.full((1, width), block_id // NSEG, jnp.int32)
        segment = lax.rem(block_id, NSEG)
        block = blocks[0, :, j, :]
        columns.append(
            jnp.concatenate([block * (segment == q).astype(jnp.float32) for q in range(NSEG)], axis=0)
        )
    smooth = jnp.dot(
        smoother[...], jnp.concatenate(columns, axis=1),
        precision=lax.Precision.HIGHEST, preferred_element_type=jnp.float32,
    )
    for m in range(n_sp):
        for j in range(listed):
            outgoing[m, j * shells : (j + 1) * shells, :] = smooth[
                m * shells : (m + 1) * shells, j * width : (j + 1) * width
            ]

    pl.semaphore_wait(barrier, n_sp - 1 + n_ev - 1)

    def label_copy(step):
        return pltpu.make_async_remote_copy(
            src_ref=label_out, dst_ref=labels.at[0, step], send_sem=label_send_sem,
            recv_sem=label_recv_sem, device_id=(ev, holder(step)), device_id_type=MESH,
        )

    def copy(step):
        return pltpu.make_async_remote_copy(
            src_ref=outgoing.at[holder(step)], dst_ref=arrived.at[0, step], send_sem=send_sem,
            recv_sem=recv_sem.at[step // size], device_id=(ev, holder(step)), device_id_type=MESH,
        )

    def send_label(step, carry):
        label_copy(step).start()
        return carry

    def send(step, carry):
        copy(step).start()
        return carry

    for group in range(groups):
        lax.fori_loop(max(group * size, 1), (group + 1) * size, send, 0)
        if group == 0:
            lax.fori_loop(1, n_sp, send_label, 0)

    arrived[0, 0] = outgoing[sp]
    labels[0, 0] = label_out[...]

    for load in loads[3:]:
        load.wait()
    shell_of = lax.broadcasted_iota(jnp.int32, (shells, width), 0)
    level = jnp.zeros((shells, width), jnp.float32)
    for r in range(shells):
        level = jnp.where(shell_of == r, levels[r].astype(jnp.float32), level)
    level = diffusion_rate * level
    lane = lax.broadcasted_iota(jnp.int32, (1, width), 1)
    right_half = lane < width // 2
    after = jnp.minimum(ev + 1, n_ev - 1)
    before = jnp.maximum(ev - 1, 0)
    inside = jnp.where(right_half, (ev + 1 < n_ev).astype(jnp.float32), (ev > 0).astype(jnp.float32))

    def tile(start, which):
        return scale[pl.ds(start, BPT), pl.ds(pl.multiple_of(which * width, width), width)]

    def coefficients(stripe, carry):
        start = pl.multiple_of(stripe * BPT, BPT)
        main = tile(start, ev)
        sides = jnp.where(right_half, tile(start, after), tile(start, before)) * inside
        coef[pl.ds(start, BPT)] = level[None] * main[:, None, :]
        beside_coef[pl.ds(start, BPT)] = level[None] * sides[:, None, :]
        return carry

    lax.fori_loop(0, n_sp, coefficients, 0)
    blank = jnp.zeros((1, shells, width), jnp.float32)
    for field in (here, there, beside_here, beside_there):
        field[0:1] = blank
        field[rows + 1 : rows + 2] = blank

    def taken(buffer, one, two, step):
        return pltpu.make_async_remote_copy(
            src_ref=buffer, dst_ref=buffer, send_sem=one, recv_sem=two,
            device_id=(peer(step), sp), device_id_type=MESH,
        )

    def passed(step, group):
        span = pl.ds(group * size, size)
        return pltpu.make_async_remote_copy(
            src_ref=arrived.at[0, span], dst_ref=arrived.at[step, span],
            send_sem=pass_send_sem.at[step, group], recv_sem=pass_recv_sem.at[step, group],
            device_id=(peer(step), sp), device_id_type=MESH,
        )

    def label_passed(step):
        return pltpu.make_async_remote_copy(
            src_ref=labels.at[0], dst_ref=labels.at[step],
            send_sem=label_pass_send_sem.at[step], recv_sem=label_pass_recv_sem.at[step],
            device_id=(peer(step), sp), device_id_type=MESH,
        )

    side_tile = jnp.where(right_half, ev + 1, ev - 1) * BPT

    def place(sources, first):
        def one(slot, carry):
            start = lax.rem(sp - slot + n_sp, n_sp) * BPT + 1
            if first:
                main = [jnp.zeros((shells, width), jnp.float32) for _ in range(BPT)]
                sides = list(main)
            else:
                main = [here[start + k] for k in range(BPT)]
                sides = [beside_here[start + k] for k in range(BPT)]
            for source in sources:
                for j in range(listed):
                    block = arrived[source, slot, j * shells : (j + 1) * shells, :]
                    label = jnp.broadcast_to(labels[source, slot, j : j + 1, :], (shells, width))
                    in_main = label - ev * BPT
                    in_sides = label - side_tile
                    for k in range(BPT):
                        main[k] = main[k] + jnp.where(in_main == k, block, 0.0)
                        sides[k] = sides[k] + jnp.where(in_sides == k, block, 0.0)
            for k in range(BPT):
                here[start + k] = main[k]
                beside_here[start + k] = sides[k]
            return carry

        return one

    label_span = labels.at[0, pl.ds(0, n_sp - 1)]
    for group in range(groups):
        count = size - 1 if group == 0 else size
        taken(arrived.at[0, pl.ds(0, count)], send_sem, recv_sem.at[group], 1).wait_recv()
        for step in range(1, n_ev):
            passed(step, group).start()
        if group == 0:
            taken(label_span, label_send_sem, label_recv_sem, 1).wait_recv()
            for step in range(1, n_ev):
                label_passed(step).start()
        lax.fori_loop(group * size, (group + 1) * size, place([0], True), 0, unroll=2)

    for step in range(1, n_ev):
        label_passed(step).wait_recv()
    for group in range(groups):
        for step in range(1, n_ev):
            passed(step, group).wait_recv()
        lax.fori_loop(group * size, (group + 1) * size, place(range(1, n_ev), False), 0, unroll=2)

    at_end = (lane == width - 1)[None]
    at_start = (lane == 0)[None]

    def diffuse(field, side_field, new_field, new_side):
        def chunk(stripe, carry):
            start = stripe * BPT
            main_rows = field[pl.ds(start, BPT + 2)]
            side_rows = side_field[pl.ds(start, BPT + 2)]
            main, sides = main_rows[1:-1], side_rows[1:-1]
            main_up, sides_up = pltpu.roll(main, width - 1, 2), pltpu.roll(sides, width - 1, 2)
            main_down, sides_down = pltpu.roll(main, 1, 2), pltpu.roll(sides, 1, 2)
            around = (
                main_rows[2:] + main_rows[:-2]
                + jnp.where(at_end, sides_up, main_up)
                + jnp.where(at_start, sides_down, main_down)
            )
            new = main + coef[pl.ds(start, BPT)] * (around - 4.0 * main)
            if new_field is None:
                for k in range(BPT):
                    final[pl.ds(start + k, shells, stride=rows), :] = new[k]
                return carry
            new_field[pl.ds(start + 1, BPT)] = new
            around = (
                side_rows[2:] + side_rows[:-2]
                + jnp.where(at_end, main_up, sides_up)
                + jnp.where(at_start, main_down, sides_down)
            )
            new_side[pl.ds(start + 1, BPT)] = sides + beside_coef[pl.ds(start, BPT)] * (around - 4.0 * sides)
            return carry

        return chunk

    now, later = (here, beside_here), (there, beside_there)
    for repeat in range(PASSES - 1):
        lax.fori_loop(0, n_sp, diffuse(*now, *later), 0, unroll=2)
        now, later = later, now
    half = rows // 2
    for part in range(2):
        lax.fori_loop(part * n_sp // 2, (part + 1) * n_sp // 2, diffuse(*now, None, None), 0, unroll=2)
        for r in range(shells):
            span = pl.ds(r * rows + part * half, half)
            pltpu.make_async_copy(final.at[span], out.at[span], store_sem).start()

    taken(label_span, label_send_sem, label_recv_sem, 1).wait_send()
    taken(arrived.at[0, pl.ds(0, n_sp - 1)], send_sem, recv_sem.at[0], 1).wait_send()
    for step in range(1, n_ev):
        label_passed(step).wait_send()
        for group in range(groups):
            passed(step, group).wait_send()
    pltpu.make_async_copy(final, out, store_sem).wait()


def solution(mesh):
    n_ev, n_sp = mesh.shape["ev"], mesh.shape["sp"]
    groups = 4

    def per_device(partial_kernels, block_ids, radial_smoother, shell_level, lateral_scale):
        listed, width = partial_kernels.shape[2:]
        shells = shell_level.shape[0]
        rows = lateral_scale.shape[0]
        field = pltpu.VMEM((rows + 2, shells, width), jnp.float32)
        inner = pltpu.VMEM((rows, shells, width), jnp.float32)
        dma = pltpu.SemaphoreType.DMA
        out = pl.pallas_call(
            functools.partial(kernel, n_ev, n_sp),
            out_shape=jax.ShapeDtypeStruct((shells * rows, width), jnp.float32),
            in_specs=[pl.BlockSpec(memory_space=pltpu.HBM)] * 5,
            out_specs=pl.BlockSpec(memory_space=pltpu.HBM),
            scratch_shapes=[
                pltpu.SMEM(block_ids.shape, jnp.int32),
                pltpu.SMEM(shell_level.shape, jnp.int32),
                pltpu.VMEM(partial_kernels.shape, jnp.float32),
                pltpu.VMEM(radial_smoother.shape, jnp.float32),
                pltpu.VMEM(lateral_scale.shape, jnp.float32),
                pltpu.VMEM((n_sp, listed * shells, width), jnp.float32),
                pltpu.VMEM((listed, width), jnp.int32),
                pltpu.VMEM((n_ev, n_sp, listed * shells, width), jnp.float32),
                pltpu.VMEM((n_ev, n_sp, listed, width), jnp.int32),
                field, field, field, field, inner, inner,
                pltpu.VMEM((shells * rows, width), jnp.float32),
                dma((5,)), dma, dma((groups,)), dma, dma,
                dma((n_ev, groups)), dma((n_ev, groups)), dma((n_ev,)), dma((n_ev,)), dma,
            ],
            compiler_params=pltpu.CompilerParams(
                collective_id=0, has_side_effects=True, vmem_limit_bytes=63 * 1024 * 1024
            ),
        )(block_ids, shell_level, partial_kernels, radial_smoother, lateral_scale)
        return out.reshape(shells, rows, width)

    placed = (P("ev", None, "sp", None), P("ev", "sp"), P(), P("sp"), P())
    return jax.shard_map(
        per_device, mesh=mesh, in_specs=placed, out_specs=P("sp", None, "ev"), check_vma=False
    )
```

```python
import functools

import jax
import jax.numpy as jnp
from jax import lax
from jax.experimental import pallas as pl
from jax.experimental.pallas import tpu as pltpu
from jax.sharding import PartitionSpec as P

BPT = 8
PASSES = 4
NSEG = 4
MESH = pl.DeviceIdType.MESH

diffusion_rate = 0.0615


def halves(value):
    high = value.astype(jnp.bfloat16)
    return high, (value - high.astype(jnp.float32)).astype(jnp.bfloat16)


def product(left, right):
    left_high, left_low = halves(left)
    right_high, right_low = halves(right)
    dot = functools.partial(jnp.dot, preferred_element_type=jnp.float32)
    return dot(left_high, right_high) + (dot(left_high, right_low) + dot(left_low, right_high))


def kernel(
    n_ev, n_sp, ids_in, levels_in, blocks_in, smoother_in, scale_in, out,
    ids, levels, blocks, smoother, scale,
    outgoing, label_out, arrived, labels, here, there, beside_here, beside_there, coef, beside_coef,
    load_sem, send_sem, recv_sem, label_send_sem, label_recv_sem,
    label_pass_send_sem, label_pass_recv_sem,
):
    ev, sp = lax.axis_index("ev"), lax.axis_index("sp")
    rows, shells, width = coef.shape
    listed = blocks.shape[2]
    groups = recv_sem.shape[0]
    size = n_sp // groups

    loads = [
        pltpu.make_async_copy(given, held, load_sem.at[i])
        for i, (given, held) in enumerate(
            [(ids_in, ids), (blocks_in, blocks), (smoother_in, smoother), (levels_in, levels), (scale_in, scale)]
        )
    ]
    for load in loads:
        load.start()

    def holder(step):
        return lax.rem(sp + step, n_sp)

    def peer(step):
        return lax.rem(ev + step, n_ev)

    barrier = pltpu.get_barrier_semaphore()

    def greet(turn, step, carry):
        pl.semaphore_signal(barrier, inc=1, device_id=(peer(turn), holder(step)), device_id_type=MESH)
        return carry

    for turn in range(n_ev):
        lax.fori_loop(int(turn == 0), n_sp, functools.partial(greet, turn), 0)

    for load in loads[:3]:
        load.wait()
    columns = []
    for j in range(listed):
        block_id = ids[0, j]
        label_out[j : j + 1, :] = jnp.full((1, width), block_id // NSEG, jnp.int32)
        segment = lax.rem(block_id, NSEG)
        block = blocks[0, :, j, :]
        columns.append(
            jnp.concatenate([block * (segment == q).astype(jnp.float32) for q in range(NSEG)], axis=0)
        )
    smooth = product(smoother[...], jnp.concatenate(columns, axis=1))
    for m in range(n_sp):
        for j in range(listed):
            outgoing[m, j * shells : (j + 1) * shells, :] = smooth[
                m * shells : (m + 1) * shells, j * width : (j + 1) * width
            ]

    pl.semaphore_wait(barrier, n_sp * n_ev - 1)

    def label_copy(step):
        return pltpu.make_async_remote_copy(
            src_ref=label_out, dst_ref=labels.at[0, step], send_sem=label_send_sem,
            recv_sem=label_recv_sem, device_id=(ev, holder(step)), device_id_type=MESH,
        )

    def copy(step, turn):
        return pltpu.make_async_remote_copy(
            src_ref=outgoing.at[holder(step)], dst_ref=arrived.at[step * n_ev + turn], send_sem=send_sem,
            recv_sem=recv_sem.at[step // size], device_id=(peer(turn), holder(step)), device_id_type=MESH,
        )

    def send_label(step, carry):
        label_copy(step).start()
        return carry

    def send(step, carry):
        for turn in range(n_ev):
            copy(step, turn).start()
        return carry

    for turn in range(1, n_ev):
        copy(0, turn).start()
    lax.fori_loop(1, size, send, 0)
    lax.fori_loop(1, n_sp, send_label, 0)
    lax.fori_loop(size, n_sp, send, 0)

    arrived[0] = outgoing[sp]
    labels[0, 0] = label_out[...]

    for load in loads[3:]:
        load.wait()
    shell_of = lax.broadcasted_iota(jnp.int32, (shells, width), 0)
    level = jnp.zeros((shells, width), jnp.float32)
    for r in range(shells):
        level = jnp.where(shell_of == r, levels[r].astype(jnp.float32), level)
    level = diffusion_rate * level
    lane = lax.broadcasted_iota(jnp.int32, (1, width), 1)
    right_half = lane < width // 2
    after = jnp.minimum(ev + 1, n_ev - 1)
    before = jnp.maximum(ev - 1, 0)
    inside = jnp.where(right_half, (ev + 1 < n_ev).astype(jnp.float32), (ev > 0).astype(jnp.float32))

    def tile(start, which):
        return scale[pl.ds(start, BPT), pl.ds(pl.multiple_of(which * width, width), width)]

    def coefficients(stripe, carry):
        start = pl.multiple_of(stripe * BPT, BPT)
        main = tile(start, ev)
        sides = jnp.where(right_half, tile(start, after), tile(start, before)) * inside
        coef[pl.ds(start, BPT)] = level[None] * main[:, None, :]
        beside_coef[pl.ds(start, BPT)] = level[None] * sides[:, None, :]
        return carry

    lax.fori_loop(0, n_sp, coefficients, 0)
    blank = jnp.zeros((1, shells, width), jnp.float32)
    for field in (here, there, beside_here, beside_there):
        field[0:1] = blank
        field[rows + 1 : rows + 2] = blank

    def taken(buffer, one, two, step):
        return pltpu.make_async_remote_copy(
            src_ref=buffer, dst_ref=buffer, send_sem=one, recv_sem=two,
            device_id=(peer(step), sp), device_id_type=MESH,
        )

    def label_passed(step):
        return pltpu.make_async_remote_copy(
            src_ref=labels.at[0], dst_ref=labels.at[step],
            send_sem=label_pass_send_sem.at[step], recv_sem=label_pass_recv_sem.at[step],
            device_id=(peer(step), sp), device_id_type=MESH,
        )

    side_tile = jnp.where(right_half, ev + 1, ev - 1) * BPT

    def place(slot, carry):
        start = lax.rem(sp - slot + n_sp, n_sp) * BPT + 1
        main = [jnp.zeros((shells, width), jnp.float32) for _ in range(BPT)]
        sides = list(main)
        for turn in range(n_ev):
            for j in range(listed):
                block = arrived[slot * n_ev + turn, j * shells : (j + 1) * shells, :]
                label = jnp.broadcast_to(labels[turn, slot, j : j + 1, :], (shells, width))
                in_main = label - ev * BPT
                in_sides = label - side_tile
                for k in range(BPT):
                    main[k] = main[k] + jnp.where(in_main == k, block, 0.0)
                    sides[k] = sides[k] + jnp.where(in_sides == k, block, 0.0)
        for k in range(BPT):
            here[start + k] = main[k]
            beside_here[start + k] = sides[k]
        return carry

    label_span = labels.at[0, pl.ds(0, n_sp - 1)]
    taken(label_span, label_send_sem, label_recv_sem, 1).wait_recv()
    for step in range(1, n_ev):
        label_passed(step).start()
    for group in range(groups):
        count = size * n_ev - (group == 0)
        taken(arrived.at[pl.ds(0, count)], send_sem, recv_sem.at[group], 1).wait_recv()
        if group == 0:
            for step in range(1, n_ev):
                label_passed(step).wait_recv()
        lax.fori_loop(group * size, (group + 1) * size, place, 0, unroll=2)

    at_end = (lane == width - 1)[None]
    at_start = (lane == 0)[None]

    def diffuse(field, side_field, new_field, new_side):
        def chunk(stripe, carry):
            start = stripe * BPT
            main_rows = field[pl.ds(start, BPT + 2)]
            side_rows = side_field[pl.ds(start, BPT + 2)]
            main, sides = main_rows[1:-1], side_rows[1:-1]
            main_up, sides_up = pltpu.roll(main, width - 1, 2), pltpu.roll(sides, width - 1, 2)
            main_down, sides_down = pltpu.roll(main, 1, 2), pltpu.roll(sides, 1, 2)
            around = (
                main_rows[2:] + main_rows[:-2]
                + jnp.where(at_end, sides_up, main_up)
                + jnp.where(at_start, sides_down, main_down)
            )
            new = main + coef[pl.ds(start, BPT)] * (around - 4.0 * main)
            if new_field is None:
                out[pl.ds(start, BPT)] = new
                return carry
            new_field[pl.ds(start + 1, BPT)] = new
            around = (
                side_rows[2:] + side_rows[:-2]
                + jnp.where(at_end, main_up, sides_up)
                + jnp.where(at_start, main_down, sides_down)
            )
            new_side[pl.ds(start + 1, BPT)] = sides + beside_coef[pl.ds(start, BPT)] * (around - 4.0 * sides)
            return carry

        return chunk

    now, later = (here, beside_here), (there, beside_there)
    for repeat in range(PASSES - 1):
        lax.fori_loop(0, n_sp, diffuse(*now, *later), 0, unroll=4)
        now, later = later, now
    lax.fori_loop(0, n_sp, diffuse(*now, None, None), 0, unroll=4)

    taken(label_span, label_send_sem, label_recv_sem, 1).wait_send()
    for step in range(1, n_ev):
        label_passed(step).wait_send()
    taken(arrived.at[pl.ds(0, n_sp * n_ev - 1)], send_sem, recv_sem.at[0], 1).wait_send()


def solution(mesh):
    n_ev, n_sp = mesh.shape["ev"], mesh.shape["sp"]
    groups = 4

    def per_device(partial_kernels, block_ids, radial_smoother, shell_level, lateral_scale):
        listed, width = partial_kernels.shape[2:]
        shells = shell_level.shape[0]
        rows = lateral_scale.shape[0]
        field = pltpu.VMEM((rows + 2, shells, width), jnp.float32)
        inner = pltpu.VMEM((rows, shells, width), jnp.float32)
        given = (block_ids, shell_level, partial_kernels, radial_smoother, lateral_scale)
        dma = pltpu.SemaphoreType.DMA
        out = pl.pallas_call(
            functools.partial(kernel, n_ev, n_sp),
            out_shape=jax.ShapeDtypeStruct((rows, shells, width), jnp.float32),
            in_specs=[pl.BlockSpec(memory_space=pltpu.HBM)] * 5,
            out_specs=pl.BlockSpec(memory_space=pltpu.VMEM),
            scratch_shapes=[
                pltpu.SMEM(block_ids.shape, jnp.int32),
                pltpu.SMEM(shell_level.shape, jnp.int32),
                pltpu.VMEM(partial_kernels.shape, jnp.float32),
                pltpu.VMEM(radial_smoother.shape, jnp.float32),
                pltpu.VMEM(lateral_scale.shape, jnp.float32),
                pltpu.VMEM((n_sp, listed * shells, width), jnp.float32),
                pltpu.VMEM((listed, width), jnp.int32),
                pltpu.VMEM((n_sp * n_ev, listed * shells, width), jnp.float32),
                pltpu.VMEM((n_ev, n_sp, listed, width), jnp.int32),
                field, field, field, field, inner, inner,
                dma((5,)), dma, dma((groups,)), dma, dma, dma((n_ev,)), dma((n_ev,)),
            ],
            compiler_params=pltpu.CompilerParams(
                collective_id=0, has_side_effects=True, vmem_limit_bytes=40 * 1024 * 1024
            ),
        )(*[pltpu.with_memory_space_constraint(x, pltpu.HBM) for x in given])
        return jnp.transpose(out, (1, 0, 2))

    placed = (P("ev", None, "sp", None), P("ev", "sp"), P(), P("sp"), P())
    return jax.shard_map(
        per_device, mesh=mesh, in_specs=placed, out_specs=P("sp", None, "ev"), check_vma=False
    )
```

```python
import functools

import jax
import jax.numpy as jnp
from jax import lax
from jax.experimental import pallas as pl
from jax.experimental.pallas import tpu as pltpu
from jax.sharding import PartitionSpec as P

BPT = 8
PASSES = 4
NSEG = 4
MESH = pl.DeviceIdType.MESH

diffusion_rate = 0.0615


def halves(value):
    high = value.astype(jnp.bfloat16)
    return high, (value - high.astype(jnp.float32)).astype(jnp.bfloat16)


def product(left, right):
    left_high, left_low = halves(left)
    right_high, right_low = halves(right)
    dot = functools.partial(jnp.dot, preferred_element_type=jnp.float32)
    return dot(left_high, right_high) + (dot(left_high, right_low) + dot(left_low, right_high))


def kernel(
    n_ev, n_sp, ids_in, levels_in, blocks_in, smoother_in, scale_in, out,
    ids, levels, blocks, smoother, scale,
    outgoing, label_out, arrived, labels, here, there, coef, strip_coef, edges, edge_labels, ends,
    load_sem, send_sem, recv_sem, label_send_sem, label_recv_sem,
    label_pass_send_sem, label_pass_recv_sem,
):
    ev, sp = lax.axis_index("ev"), lax.axis_index("sp")
    rows, shells, width = coef.shape
    listed = blocks.shape[2]
    groups = recv_sem.shape[0]
    sets = edges.shape[0]
    span = 2 * PASSES
    per_set = width // span
    size = n_sp // groups

    loads = [
        pltpu.make_async_copy(given, held, load_sem.at[i])
        for i, (given, held) in enumerate(
            [(ids_in, ids), (blocks_in, blocks), (smoother_in, smoother), (levels_in, levels), (scale_in, scale)]
        )
    ]
    for load in loads:
        load.start()

    def holder(step):
        return lax.rem(sp + step, n_sp)

    def peer(step):
        return lax.rem(ev + step, n_ev)

    barrier = pltpu.get_barrier_semaphore()

    def greet(turn, step, carry):
        pl.semaphore_signal(barrier, inc=1, device_id=(peer(turn), holder(step)), device_id_type=MESH)
        return carry

    for turn in range(n_ev):
        lax.fori_loop(int(turn == 0), n_sp, functools.partial(greet, turn), 0)

    for load in loads[:3]:
        load.wait()
    columns = []
    for j in range(listed):
        block_id = ids[0, j]
        label_out[j : j + 1, :] = jnp.full((1, width), block_id // NSEG, jnp.int32)
        segment = lax.rem(block_id, NSEG)
        block = blocks[0, :, j, :]
        columns.append(
            jnp.concatenate([block * (segment == q).astype(jnp.float32) for q in range(NSEG)], axis=0)
        )
    smooth = product(smoother[...], jnp.concatenate(columns, axis=1))
    for m in range(n_sp):
        for j in range(listed):
            outgoing[m, j * shells : (j + 1) * shells, :] = smooth[
                m * shells : (m + 1) * shells, j * width : (j + 1) * width
            ]

    pl.semaphore_wait(barrier, n_sp * n_ev - 1)

    def label_copy(step):
        return pltpu.make_async_remote_copy(
            src_ref=label_out, dst_ref=labels.at[0, step], send_sem=label_send_sem,
            recv_sem=label_recv_sem, device_id=(ev, holder(step)), device_id_type=MESH,
        )

    def copy(step, turn):
        return pltpu.make_async_remote_copy(
            src_ref=outgoing.at[holder(step)], dst_ref=arrived.at[step * n_ev + turn], send_sem=send_sem,
            recv_sem=recv_sem.at[step // size], device_id=(peer(turn), holder(step)), device_id_type=MESH,
        )

    def send_label(step, carry):
        label_copy(step).start()
        return carry

    def send(step, carry):
        for turn in range(n_ev):
            copy(step, turn).start()
        return carry

    for turn in range(1, n_ev):
        copy(0, turn).start()
    lax.fori_loop(1, size, send, 0)
    lax.fori_loop(1, n_sp, send_label, 0)
    lax.fori_loop(size, n_sp, send, 0)

    arrived[0] = outgoing[sp]
    labels[0, 0] = label_out[...]

    for load in loads[3:]:
        load.wait()
    shell_of = lax.broadcasted_iota(jnp.int32, (shells, width), 0)
    level = jnp.zeros((shells, width), jnp.float32)
    for r in range(shells):
        level = jnp.where(shell_of == r, levels[r].astype(jnp.float32), level)
    level = diffusion_rate * level
    lane = lax.broadcasted_iota(jnp.int32, (1, width), 1)
    spot = lane & (span - 1)
    group_of = lax.shift_right_logical(lane, span.bit_length() - 1)
    late_half = lane >= width // 2
    after = jnp.minimum(ev + 1, n_ev - 1)
    before = jnp.maximum(ev - 1, 0)
    has_after = (ev + 1 < n_ev).astype(jnp.float32)
    has_before = (ev > 0).astype(jnp.float32)

    def tile(start, which):
        return scale[pl.ds(start, BPT), pl.ds(pl.multiple_of(which * width, width), width)]

    left_scale = [jnp.zeros((BPT, width), jnp.float32)] * sets
    right_scale = list(left_scale)
    for stripe in range(n_sp):
        start = stripe * BPT
        main = tile(start, ev)
        coef[pl.ds(start, BPT)] = level[None] * main[:, None, :]
        which, local = divmod(stripe, per_set)
        shift = (local * span + PASSES) % width
        left = jnp.where(late_half, tile(start, before) * has_before, main)
        right = jnp.where(late_half, main, tile(start, after) * has_after)
        mine = group_of == local
        left_scale[which] = jnp.where(mine, pltpu.roll(left, shift, 1), left_scale[which])
        right_scale[which] = jnp.where(mine, pltpu.roll(right, shift, 1), right_scale[which])
    for which in range(sets):
        strip_coef[0, which] = level[None] * left_scale[which][:, None, :]
        strip_coef[1, which] = level[None] * right_scale[which][:, None, :]
        for entry in range(n_ev * listed):
            edges[which, entry] = jnp.zeros((shells, width), jnp.float32)
            edge_labels[which, entry] = jnp.full((shells, width), -n_ev * n_sp * BPT * span, jnp.int32)

    blank = jnp.zeros((1, shells, width), jnp.float32)
    for field in (here, there):
        field[0:1] = blank
        field[rows + 1 : rows + 2] = blank

    def taken(buffer, one, two, step):
        return pltpu.make_async_remote_copy(
            src_ref=buffer, dst_ref=buffer, send_sem=one, recv_sem=two,
            device_id=(peer(step), sp), device_id_type=MESH,
        )

    def label_passed(step):
        return pltpu.make_async_remote_copy(
            src_ref=labels.at[0], dst_ref=labels.at[step],
            send_sem=label_pass_send_sem.at[step], recv_sem=label_pass_recv_sem.at[step],
            device_id=(peer(step), sp), device_id_type=MESH,
        )

    def place(slot, carry):
        stripe = lax.rem(sp - slot + n_sp, n_sp)
        start = stripe * BPT + 1
        which, local = stripe // per_set, lax.rem(stripe, per_set)
        shift = lax.rem(local * span + PASSES, width)
        mine = group_of == local
        main = [jnp.zeros((shells, width), jnp.float32) for _ in range(BPT)]
        for turn in range(n_ev):
            for j in range(listed):
                block = arrived[slot * n_ev + turn, j * shells : (j + 1) * shells, :]
                label = jnp.broadcast_to(labels[turn, slot, j : j + 1, :], (shells, width))
                entry = turn * listed + j
                edges[which, entry] = jnp.where(mine, pltpu.roll(block, shift, 1), edges[which, entry])
                edge_labels[which, entry] = jnp.where(mine, label, edge_labels[which, entry])
                in_main = label - ev * BPT
                for k in range(BPT):
                    main[k] = main[k] + jnp.where(in_main == k, block, 0.0)
        for k in range(BPT):
            here[start + k] = main[k]
        return carry

    label_span = labels.at[0, pl.ds(0, n_sp - 1)]
    taken(label_span, label_send_sem, label_recv_sem, 1).wait_recv()
    for step in range(1, n_ev):
        label_passed(step).start()
    for group in range(groups):
        count = size * n_ev - (group == 0)
        taken(arrived.at[pl.ds(0, count)], send_sem, recv_sem.at[group], 1).wait_recv()
        if group == 0:
            for step in range(1, n_ev):
                label_passed(step).wait_recv()
        lax.fori_loop(group * size, (group + 1) * size, place, 0, unroll=2)

    def strip_of(inner, outer):
        base = jnp.where(spot < PASSES, inner, outer) * BPT
        strip = []
        for which in range(sets):
            found = [edge_labels[which, entry] - base for entry in range(n_ev * listed)]
            values = [edges[which, entry] for entry in range(n_ev * listed)]
            strip.append([
                sum(jnp.where(at == k, value, 0.0) for at, value in zip(found, values)) for k in range(BPT)
            ])
        return strip

    def across(strip, which, back):
        k, far = (BPT - 1, 0) if back else (0, per_set - 1)
        shift = span if back else width - span
        beyond = which - 1 if back else which + 1
        rolled = pltpu.roll(strip[which][k], shift, 1)
        outside = pltpu.roll(strip[beyond][k], shift, 1) if 0 <= beyond < sets else 0.0
        return jnp.where(group_of == far, outside, rolled)

    def strip_pass(strip, side):
        new = []
        for which in range(sets):
            new.append([])
            for k in range(BPT):
                cell = strip[which][k]
                up = strip[which][k + 1] if k < BPT - 1 else across(strip, which, False)
                down = strip[which][k - 1] if k > 0 else across(strip, which, True)
                around = up + down + pltpu.roll(cell, width - 1, 1) + pltpu.roll(cell, 1, 1)
                new[which].append(cell + strip_coef[side, which, k] * (around - 4.0 * cell))
        return new

    left, right = strip_of(ev - 1, ev), strip_of(ev, ev + 1)
    for repeat in range(PASSES):
        for which in range(sets):
            for k in range(BPT):
                ends[repeat, which, k] = jnp.where(
                    spot == 0,
                    pltpu.roll(left[which][k], width - PASSES + 1, 1),
                    pltpu.roll(right[which][k], width - PASSES - 1, 1),
                )
        if repeat < PASSES - 1:
            left, right = strip_pass(left, 0), strip_pass(right, 1)

    at_end = (lane == width - 1)[None]
    at_start = (lane == 0)[None]

    def diffuse(repeat, field, new_field):
        def chunk(stripe, carry):
            start = stripe * BPT
            main_rows = field[pl.ds(start, BPT + 2)]
            main = main_rows[1:-1]
            shift = lax.rem(width - lax.rem(stripe, per_set) * span, width)
            outside = pltpu.roll(ends[repeat, stripe // per_set], shift, 2)
            around = (
                main_rows[2:] + main_rows[:-2]
                + jnp.where(at_end, outside, pltpu.roll(main, width - 1, 2))
                + jnp.where(at_start, outside, pltpu.roll(main, 1, 2))
            )
            new = main + coef[pl.ds(start, BPT)] * (around - 4.0 * main)
            if new_field is None:
                out[pl.ds(start, BPT)] = new
            else:
                new_field[pl.ds(start + 1, BPT)] = new
            return carry

        return chunk

    now, later = here, there
    for repeat in range(PASSES):
        last = repeat == PASSES - 1
        lax.fori_loop(0, n_sp, diffuse(repeat, now, None if last else later), 0, unroll=4)
        now, later = later, now

    taken(label_span, label_send_sem, label_recv_sem, 1).wait_send()
    for step in range(1, n_ev):
        label_passed(step).wait_send()
    taken(arrived.at[pl.ds(0, n_sp * n_ev - 1)], send_sem, recv_sem.at[0], 1).wait_send()


def solution(mesh):
    n_ev, n_sp = mesh.shape["ev"], mesh.shape["sp"]
    groups = 4

    def per_device(partial_kernels, block_ids, radial_smoother, shell_level, lateral_scale):
        listed, width = partial_kernels.shape[2:]
        shells = shell_level.shape[0]
        rows = lateral_scale.shape[0]
        sets = n_sp // (width // (2 * PASSES))
        field = pltpu.VMEM((rows + 2, shells, width), jnp.float32)
        inner = pltpu.VMEM((rows, shells, width), jnp.float32)
        given = (block_ids, shell_level, partial_kernels, radial_smoother, lateral_scale)
        dma = pltpu.SemaphoreType.DMA
        out = pl.pallas_call(
            functools.partial(kernel, n_ev, n_sp),
            out_shape=jax.ShapeDtypeStruct((rows, shells, width), jnp.float32),
            in_specs=[pl.BlockSpec(memory_space=pltpu.HBM)] * 5,
            out_specs=pl.BlockSpec(memory_space=pltpu.VMEM),
            scratch_shapes=[
                pltpu.SMEM(block_ids.shape, jnp.int32),
                pltpu.SMEM(shell_level.shape, jnp.int32),
                pltpu.VMEM(partial_kernels.shape, jnp.float32),
                pltpu.VMEM(radial_smoother.shape, jnp.float32),
                pltpu.VMEM(lateral_scale.shape, jnp.float32),
                pltpu.VMEM((n_sp, listed * shells, width), jnp.float32),
                pltpu.VMEM((listed, width), jnp.int32),
                pltpu.VMEM((n_sp * n_ev, listed * shells, width), jnp.float32),
                pltpu.VMEM((n_ev, n_sp, listed, width), jnp.int32),
                field, field, inner,
                pltpu.VMEM((2, sets, BPT, shells, width), jnp.float32),
                pltpu.VMEM((sets, n_ev * listed, shells, width), jnp.float32),
                pltpu.VMEM((sets, n_ev * listed, shells, width), jnp.int32),
                pltpu.VMEM((PASSES, sets, BPT, shells, width), jnp.float32),
                dma((5,)), dma, dma((groups,)), dma, dma, dma((n_ev,)), dma((n_ev,)),
            ],
            compiler_params=pltpu.CompilerParams(
                collective_id=0, has_side_effects=True, vmem_limit_bytes=40 * 1024 * 1024
            ),
        )(*[pltpu.with_memory_space_constraint(x, pltpu.HBM) for x in given])
        return jnp.transpose(out, (1, 0, 2))

    placed = (P("ev", None, "sp", None), P("ev", "sp"), P(), P("sp"), P())
    return jax.shard_map(
        per_device, mesh=mesh, in_specs=placed, out_specs=P("sp", None, "ev"), check_vma=False
    )
```

```python
import functools

import jax
import jax.numpy as jnp
from jax import lax
from jax.experimental import pallas as pl
from jax.experimental.pallas import tpu as pltpu
from jax.sharding import PartitionSpec as P

BPT = 8
PASSES = 4
NSEG = 4
MESH = pl.DeviceIdType.MESH

diffusion_rate = 0.0615


def halves(value):
    high = value.astype(jnp.bfloat16)
    return high, (value - high.astype(jnp.float32)).astype(jnp.bfloat16)


def product(left, right):
    left_high, left_low = halves(left)
    right_high, right_low = halves(right)
    dot = functools.partial(jnp.dot, preferred_element_type=jnp.float32)
    return dot(left_high, right_high) + (dot(left_high, right_low) + dot(left_low, right_high))


def kernel(
    n_ev, n_sp, ids_in, levels_in, blocks_in, smoother_in, scale_in, out,
    ids, levels, blocks, smoother, scale,
    outgoing, label_out, arrived, labels, here, there, coef, strip_coef, edges, edge_labels, ends,
    load_sem, send_sem, recv_sem, label_send_sem, label_recv_sem,
    label_pass_send_sem, label_pass_recv_sem,
):
    ev, sp = lax.axis_index("ev"), lax.axis_index("sp")
    rows, shells, width = coef.shape
    listed = blocks.shape[2]
    groups = recv_sem.shape[0]
    sets = edges.shape[0]
    span = 2 * PASSES
    per_set = width // span
    size = n_sp // groups

    loads = [
        pltpu.make_async_copy(given, held, load_sem.at[i])
        for i, (given, held) in enumerate(
            [(ids_in, ids), (blocks_in, blocks), (smoother_in, smoother), (levels_in, levels), (scale_in, scale)]
        )
    ]
    for load in loads:
        load.start()

    def holder(step):
        return lax.rem(sp + step, n_sp)

    def peer(step):
        return lax.rem(ev + step, n_ev)

    barrier = pltpu.get_barrier_semaphore()

    def greet(turn, step, carry):
        pl.semaphore_signal(barrier, inc=1, device_id=(peer(turn), holder(step)), device_id_type=MESH)
        return carry

    for turn in range(n_ev):
        lax.fori_loop(int(turn == 0), n_sp, functools.partial(greet, turn), 0)

    for load in loads[:3]:
        load.wait()
    columns = []
    for j in range(listed):
        block_id = ids[0, j]
        label_out[j : j + 1, :] = jnp.full((1, width), block_id // NSEG, jnp.int32)
        segment = lax.rem(block_id, NSEG)
        block = blocks[0, :, j, :]
        columns.append(
            jnp.concatenate([block * (segment == q).astype(jnp.float32) for q in range(NSEG)], axis=0)
        )
    smooth = product(smoother[...], jnp.concatenate(columns, axis=1))
    for m in range(n_sp):
        for j in range(listed):
            outgoing[m, j * shells : (j + 1) * shells, :] = smooth[
                m * shells : (m + 1) * shells, j * width : (j + 1) * width
            ]

    pl.semaphore_wait(barrier, n_sp * n_ev - 1)

    def label_copy(step):
        return pltpu.make_async_remote_copy(
            src_ref=label_out, dst_ref=labels.at[0, step], send_sem=label_send_sem,
            recv_sem=label_recv_sem, device_id=(ev, holder(step)), device_id_type=MESH,
        )

    def copy(step, turn):
        return pltpu.make_async_remote_copy(
            src_ref=outgoing.at[holder(step)], dst_ref=arrived.at[step * n_ev + turn], send_sem=send_sem,
            recv_sem=recv_sem.at[step // size], device_id=(peer(turn), holder(step)), device_id_type=MESH,
        )

    def send_label(step, carry):
        label_copy(step).start()
        return carry

    def send(step, carry):
        for turn in range(n_ev):
            copy(step, turn).start()
        return carry

    order = [groups // 2, *range(groups // 2 + 1, groups), *range(groups // 2 - 1, -1, -1)]
    for group in order:
        lax.fori_loop(max(group * size, 1), (group + 1) * size, send, 0)
        if group == order[0]:
            lax.fori_loop(1, n_sp, send_label, 0)
    for turn in range(1, n_ev):
        copy(0, turn).start()

    arrived[0] = outgoing[sp]
    labels[0, 0] = label_out[...]

    for load in loads[3:]:
        load.wait()
    shell_of = lax.broadcasted_iota(jnp.int32, (shells, width), 0)
    level = jnp.zeros((shells, width), jnp.float32)
    for r in range(shells):
        level = jnp.where(shell_of == r, levels[r].astype(jnp.float32), level)
    level = diffusion_rate * level
    lane = lax.broadcasted_iota(jnp.int32, (1, width), 1)
    spot = lane & (span - 1)
    group_of = lax.shift_right_logical(lane, span.bit_length() - 1)
    late_half = lane >= width // 2
    after = jnp.minimum(ev + 1, n_ev - 1)
    before = jnp.maximum(ev - 1, 0)
    has_after = (ev + 1 < n_ev).astype(jnp.float32)
    has_before = (ev > 0).astype(jnp.float32)

    def tile(start, which):
        return scale[pl.ds(start, BPT), pl.ds(pl.multiple_of(which * width, width), width)]

    left_scale = [jnp.zeros((BPT, width), jnp.float32)] * sets
    right_scale = list(left_scale)
    for stripe in range(n_sp):
        start = stripe * BPT
        main = tile(start, ev)
        coef[pl.ds(start, BPT)] = level[None] * main[:, None, :]
        which, local = divmod(stripe, per_set)
        shift = (local * span + PASSES) % width
        left = jnp.where(late_half, tile(start, before) * has_before, main)
        right = jnp.where(late_half, main, tile(start, after) * has_after)
        mine = group_of == local
        left_scale[which] = jnp.where(mine, pltpu.roll(left, shift, 1), left_scale[which])
        right_scale[which] = jnp.where(mine, pltpu.roll(right, shift, 1), right_scale[which])
    for which in range(sets):
        strip_coef[0, which] = level[None] * left_scale[which][:, None, :]
        strip_coef[1, which] = level[None] * right_scale[which][:, None, :]
        for entry in range(n_ev * listed):
            edges[which, entry] = jnp.zeros((shells, width), jnp.float32)
            edge_labels[which, entry] = jnp.full((shells, width), -n_ev * n_sp * BPT * span, jnp.int32)

    blank = jnp.zeros((1, shells, width), jnp.float32)
    for field in (here, there):
        field[0:1] = blank
        field[rows + 1 : rows + 2] = blank

    def taken(buffer, one, two, step):
        return pltpu.make_async_remote_copy(
            src_ref=buffer, dst_ref=buffer, send_sem=one, recv_sem=two,
            device_id=(peer(step), sp), device_id_type=MESH,
        )

    def label_passed(step):
        return pltpu.make_async_remote_copy(
            src_ref=labels.at[0], dst_ref=labels.at[step],
            send_sem=label_pass_send_sem.at[step], recv_sem=label_pass_recv_sem.at[step],
            device_id=(peer(step), sp), device_id_type=MESH,
        )

    def place(slot, carry):
        stripe = lax.rem(sp - slot + n_sp, n_sp)
        start = stripe * BPT + 1
        which, local = stripe // per_set, lax.rem(stripe, per_set)
        shift = lax.rem(local * span + PASSES, width)
        mine = group_of == local
        main = [jnp.zeros((shells, width), jnp.float32) for _ in range(BPT)]
        for turn in range(n_ev):
            for j in range(listed):
                block = arrived[slot * n_ev + turn, j * shells : (j + 1) * shells, :]
                label = jnp.broadcast_to(labels[turn, slot, j : j + 1, :], (shells, width))
                entry = turn * listed + j
                edges[which, entry] = jnp.where(mine, pltpu.roll(block, shift, 1), edges[which, entry])
                edge_labels[which, entry] = jnp.where(mine, label, edge_labels[which, entry])
                in_main = label - ev * BPT
                for k in range(BPT):
                    main[k] = main[k] + jnp.where(in_main == k, block, 0.0)
        for k in range(BPT):
            here[start + k] = main[k]
        return carry

    label_span = labels.at[0, pl.ds(0, n_sp - 1)]
    taken(label_span, label_send_sem, label_recv_sem, 1).wait_recv()
    for step in range(1, n_ev):
        label_passed(step).start()
    for group in order:
        count = size * n_ev - (group == 0)
        taken(arrived.at[pl.ds(0, count)], send_sem, recv_sem.at[group], 1).wait_recv()
        if group == order[0]:
            for step in range(1, n_ev):
                label_passed(step).wait_recv()
        lax.fori_loop(group * size, (group + 1) * size, place, 0, unroll=2)

    def strip_of(inner, outer):
        base = jnp.where(spot < PASSES, inner, outer) * BPT
        strip = []
        for which in range(sets):
            found = [edge_labels[which, entry] - base for entry in range(n_ev * listed)]
            values = [edges[which, entry] for entry in range(n_ev * listed)]
            strip.append([
                sum(jnp.where(at == k, value, 0.0) for at, value in zip(found, values)) for k in range(BPT)
            ])
        return strip

    def across(strip, which, back):
        k, far = (BPT - 1, 0) if back else (0, per_set - 1)
        shift = span if back else width - span
        beyond = which - 1 if back else which + 1
        rolled = pltpu.roll(strip[which][k], shift, 1)
        outside = pltpu.roll(strip[beyond][k], shift, 1) if 0 <= beyond < sets else 0.0
        return jnp.where(group_of == far, outside, rolled)

    def strip_pass(strip, side):
        new = []
        for which in range(sets):
            new.append([])
            for k in range(BPT):
                cell = strip[which][k]
                up = strip[which][k + 1] if k < BPT - 1 else across(strip, which, False)
                down = strip[which][k - 1] if k > 0 else across(strip, which, True)
                around = up + down + pltpu.roll(cell, width - 1, 1) + pltpu.roll(cell, 1, 1)
                new[which].append(cell + strip_coef[side, which, k] * (around - 4.0 * cell))
        return new

    left, right = strip_of(ev - 1, ev), strip_of(ev, ev + 1)
    for repeat in range(PASSES):
        for which in range(sets):
            for k in range(BPT):
                ends[repeat, which, k] = jnp.where(
                    spot == 0,
                    pltpu.roll(left[which][k], width - PASSES + 1, 1),
                    pltpu.roll(right[which][k], width - PASSES - 1, 1),
                )
        if repeat < PASSES - 1:
            left, right = strip_pass(left, 0), strip_pass(right, 1)

    at_end = (lane == width - 1)[None]
    at_start = (lane == 0)[None]

    def diffuse(repeat, field, new_field):
        def chunk(stripe, carry):
            start = stripe * BPT
            main_rows = field[pl.ds(start, BPT + 2)]
            main = main_rows[1:-1]
            shift = lax.rem(width - lax.rem(stripe, per_set) * span, width)
            outside = pltpu.roll(ends[repeat, stripe // per_set], shift, 2)
            around = (
                main_rows[2:] + main_rows[:-2]
                + jnp.where(at_end, outside, pltpu.roll(main, width - 1, 2))
                + jnp.where(at_start, outside, pltpu.roll(main, 1, 2))
            )
            new = main + coef[pl.ds(start, BPT)] * (around - 4.0 * main)
            if new_field is None:
                out[pl.ds(start, BPT)] = new
            else:
                new_field[pl.ds(start + 1, BPT)] = new
            return carry

        return chunk

    now, later = here, there
    for repeat in range(PASSES):
        last = repeat == PASSES - 1
        lax.fori_loop(0, n_sp, diffuse(repeat, now, None if last else later), 0, unroll=4)
        now, later = later, now

    taken(label_span, label_send_sem, label_recv_sem, 1).wait_send()
    for step in range(1, n_ev):
        label_passed(step).wait_send()
    taken(arrived.at[pl.ds(0, n_sp * n_ev - 1)], send_sem, recv_sem.at[0], 1).wait_send()


def solution(mesh):
    n_ev, n_sp = mesh.shape["ev"], mesh.shape["sp"]
    groups = 4

    def per_device(partial_kernels, block_ids, radial_smoother, shell_level, lateral_scale):
        listed, width = partial_kernels.shape[2:]
        shells = shell_level.shape[0]
        rows = lateral_scale.shape[0]
        sets = n_sp // (width // (2 * PASSES))
        field = pltpu.VMEM((rows + 2, shells, width), jnp.float32)
        inner = pltpu.VMEM((rows, shells, width), jnp.float32)
        given = (block_ids, shell_level, partial_kernels, radial_smoother, lateral_scale)
        dma = pltpu.SemaphoreType.DMA
        out = pl.pallas_call(
            functools.partial(kernel, n_ev, n_sp),
            out_shape=jax.ShapeDtypeStruct((rows, shells, width), jnp.float32),
            in_specs=[pl.BlockSpec(memory_space=pltpu.HBM)] * 5,
            out_specs=pl.BlockSpec(memory_space=pltpu.VMEM),
            scratch_shapes=[
                pltpu.SMEM(block_ids.shape, jnp.int32),
                pltpu.SMEM(shell_level.shape, jnp.int32),
                pltpu.VMEM(partial_kernels.shape, jnp.float32),
                pltpu.VMEM(radial_smoother.shape, jnp.float32),
                pltpu.VMEM(lateral_scale.shape, jnp.float32),
                pltpu.VMEM((n_sp, listed * shells, width), jnp.float32),
                pltpu.VMEM((listed, width), jnp.int32),
                pltpu.VMEM((n_sp * n_ev, listed * shells, width), jnp.float32),
                pltpu.VMEM((n_ev, n_sp, listed, width), jnp.int32),
                field, field, inner,
                pltpu.VMEM((2, sets, BPT, shells, width), jnp.float32),
                pltpu.VMEM((sets, n_ev * listed, shells, width), jnp.float32),
                pltpu.VMEM((sets, n_ev * listed, shells, width), jnp.int32),
                pltpu.VMEM((PASSES, sets, BPT, shells, width), jnp.float32),
                dma((5,)), dma, dma((groups,)), dma, dma, dma((n_ev,)), dma((n_ev,)),
            ],
            compiler_params=pltpu.CompilerParams(
                collective_id=0, has_side_effects=True, vmem_limit_bytes=40 * 1024 * 1024
            ),
        )(*[pltpu.with_memory_space_constraint(x, pltpu.HBM) for x in given])
        return jnp.transpose(out, (1, 0, 2))

    placed = (P("ev", None, "sp", None), P("ev", "sp"), P(), P("sp"), P())
    return jax.shard_map(
        per_device, mesh=mesh, in_specs=placed, out_specs=P("sp", None, "ev"), check_vma=False
    )
```

```python
import functools

import jax
import jax.numpy as jnp
from jax import lax
from jax.experimental import pallas as pl
from jax.experimental.pallas import tpu as pltpu
from jax.sharding import PartitionSpec as P

BPT = 8
PASSES = 4
NSEG = 4
MESH = pl.DeviceIdType.MESH

diffusion_rate = 0.0615


def halves(value):
    high = value.astype(jnp.bfloat16)
    return high, (value - high.astype(jnp.float32)).astype(jnp.bfloat16)


def product(left, right):
    left_high, left_low = halves(left)
    right_high, right_low = halves(right)
    dot = functools.partial(jnp.dot, preferred_element_type=jnp.float32)
    return dot(left_high, right_high) + (dot(left_high, right_low) + dot(left_low, right_high))


def kernel(
    n_ev, n_sp, ids_in, levels_in, blocks_in, smoother_in, scale_in, out,
    ids, levels, blocks, smoother, scale,
    outgoing, label_out, arrived, labels, here, there, coef, strip_coef, edges, edge_labels, ends,
    load_sem, send_sem, recv_sem, label_send_sem, label_recv_sem,
    label_pass_send_sem, label_pass_recv_sem,
):
    ev, sp = lax.axis_index("ev"), lax.axis_index("sp")
    rows, shells, width = coef.shape
    listed = blocks.shape[2]
    size = recv_sem.shape[0]
    groups = n_sp // size
    sets = edges.shape[0]
    span = 2 * PASSES
    per_set = width // span

    loads = [
        pltpu.make_async_copy(given, held, load_sem.at[i])
        for i, (given, held) in enumerate(
            [(ids_in, ids), (blocks_in, blocks), (smoother_in, smoother), (levels_in, levels), (scale_in, scale)]
        )
    ]
    for load in loads:
        load.start()

    def holder(step):
        return lax.rem(sp + step, n_sp)

    def peer(step):
        return lax.rem(ev + step, n_ev)

    barrier = pltpu.get_barrier_semaphore()

    def greet(turn, step, carry):
        pl.semaphore_signal(barrier, inc=1, device_id=(peer(turn), holder(step)), device_id_type=MESH)
        return carry

    for turn in range(n_ev):
        lax.fori_loop(int(turn == 0), n_sp, functools.partial(greet, turn), 0)

    for load in loads[:3]:
        load.wait()
    columns = []
    for j in range(listed):
        block_id = ids[0, j]
        label_out[j : j + 1, :] = jnp.full((1, width), block_id // NSEG, jnp.int32)
        segment = lax.rem(block_id, NSEG)
        block = blocks[0, :, j, :]
        columns.append(
            jnp.concatenate([block * (segment == q).astype(jnp.float32) for q in range(NSEG)], axis=0)
        )
    smooth = product(smoother[...], jnp.concatenate(columns, axis=1))
    for m in range(n_sp):
        for j in range(listed):
            outgoing[m, j * shells : (j + 1) * shells, :] = smooth[
                m * shells : (m + 1) * shells, j * width : (j + 1) * width
            ]

    pl.semaphore_wait(barrier, n_sp * n_ev - 1)

    def label_copy(step):
        return pltpu.make_async_remote_copy(
            src_ref=label_out, dst_ref=labels.at[0, step], send_sem=label_send_sem,
            recv_sem=label_recv_sem, device_id=(ev, holder(step)), device_id_type=MESH,
        )

    def copy(step, turn):
        return pltpu.make_async_remote_copy(
            src_ref=outgoing.at[holder(step)], dst_ref=arrived.at[step * n_ev + turn], send_sem=send_sem,
            recv_sem=recv_sem.at[lax.rem(step, size)], device_id=(peer(turn), holder(step)), device_id_type=MESH,
        )

    def send_label(step, carry):
        label_copy(step).start()
        return carry

    order = [*range(groups // 2, groups), *range(groups // 2)]

    def send(turn_of, carry):
        for quarter in order:
            for turn in range(n_ev):
                copy(quarter * size + turn_of, turn).start()
        return carry

    lax.fori_loop(1, n_sp, send_label, 0)
    for quarter in order:
        for turn in range(int(quarter == 0), n_ev):
            copy(jnp.int32(quarter * size), turn).start()
    lax.fori_loop(1, size, send, 0)

    arrived[0] = outgoing[sp]
    labels[0, 0] = label_out[...]

    for load in loads[3:]:
        load.wait()
    shell_of = lax.broadcasted_iota(jnp.int32, (shells, width), 0)
    level = jnp.zeros((shells, width), jnp.float32)
    for r in range(shells):
        level = jnp.where(shell_of == r, levels[r].astype(jnp.float32), level)
    level = diffusion_rate * level
    lane = lax.broadcasted_iota(jnp.int32, (1, width), 1)
    spot = lane & (span - 1)
    group_of = lax.shift_right_logical(lane, span.bit_length() - 1)
    late_half = lane >= width // 2
    after = jnp.minimum(ev + 1, n_ev - 1)
    before = jnp.maximum(ev - 1, 0)
    has_after = (ev + 1 < n_ev).astype(jnp.float32)
    has_before = (ev > 0).astype(jnp.float32)

    def tile(start, which):
        return scale[pl.ds(start, BPT), pl.ds(pl.multiple_of(which * width, width), width)]

    left_scale = [jnp.zeros((BPT, width), jnp.float32)] * sets
    right_scale = list(left_scale)
    for stripe in range(n_sp):
        start = stripe * BPT
        main = tile(start, ev)
        coef[pl.ds(start, BPT)] = level[None] * main[:, None, :]
        which, local = divmod(stripe, per_set)
        shift = (local * span + PASSES) % width
        left = jnp.where(late_half, tile(start, before) * has_before, main)
        right = jnp.where(late_half, main, tile(start, after) * has_after)
        mine = group_of == local
        left_scale[which] = jnp.where(mine, pltpu.roll(left, shift, 1), left_scale[which])
        right_scale[which] = jnp.where(mine, pltpu.roll(right, shift, 1), right_scale[which])
    for which in range(sets):
        strip_coef[0, which] = level[None] * left_scale[which][:, None, :]
        strip_coef[1, which] = level[None] * right_scale[which][:, None, :]
        for entry in range(n_ev * listed):
            edges[which, entry] = jnp.zeros((shells, width), jnp.float32)
            edge_labels[which, entry] = jnp.full((shells, width), -n_ev * n_sp * BPT * span, jnp.int32)

    blank = jnp.zeros((1, shells, width), jnp.float32)
    for field in (here, there):
        field[0:1] = blank
        field[rows + 1 : rows + 2] = blank

    def taken(buffer, one, two, step):
        return pltpu.make_async_remote_copy(
            src_ref=buffer, dst_ref=buffer, send_sem=one, recv_sem=two,
            device_id=(peer(step), sp), device_id_type=MESH,
        )

    def label_passed(step):
        return pltpu.make_async_remote_copy(
            src_ref=labels.at[0], dst_ref=labels.at[step],
            send_sem=label_pass_send_sem.at[step], recv_sem=label_pass_recv_sem.at[step],
            device_id=(peer(step), sp), device_id_type=MESH,
        )

    def place(group, quarter, carry):
        slot = quarter * size + group
        stripe = lax.rem(sp - slot + n_sp, n_sp)
        start = stripe * BPT + 1
        which, local = stripe // per_set, lax.rem(stripe, per_set)
        shift = lax.rem(local * span + PASSES, width)
        mine = group_of == local
        main = [jnp.zeros((shells, width), jnp.float32) for _ in range(BPT)]
        for turn in range(n_ev):
            for j in range(listed):
                block = arrived[slot * n_ev + turn, j * shells : (j + 1) * shells, :]
                label = jnp.broadcast_to(labels[turn, slot, j : j + 1, :], (shells, width))
                entry = turn * listed + j
                edges[which, entry] = jnp.where(mine, pltpu.roll(block, shift, 1), edges[which, entry])
                edge_labels[which, entry] = jnp.where(mine, label, edge_labels[which, entry])
                in_main = label - ev * BPT
                for k in range(BPT):
                    main[k] = main[k] + jnp.where(in_main == k, block, 0.0)
        for k in range(BPT):
            here[start + k] = main[k]
        return carry

    label_span = labels.at[0, pl.ds(0, n_sp - 1)]
    taken(label_span, label_send_sem, label_recv_sem, 1).wait_recv()
    for step in range(1, n_ev):
        label_passed(step).start()
    for group in range(size):
        count = groups * n_ev - (group == 0)
        taken(arrived.at[pl.ds(0, count)], send_sem, recv_sem.at[group], 1).wait_recv()
        if group == 0:
            for step in range(1, n_ev):
                label_passed(step).wait_recv()
        lax.fori_loop(0, groups, functools.partial(place, group), 0, unroll=2)

    def strip_of(inner, outer):
        base = jnp.where(spot < PASSES, inner, outer) * BPT
        strip = []
        for which in range(sets):
            found = [edge_labels[which, entry] - base for entry in range(n_ev * listed)]
            values = [edges[which, entry] for entry in range(n_ev * listed)]
            strip.append([
                sum(jnp.where(at == k, value, 0.0) for at, value in zip(found, values)) for k in range(BPT)
            ])
        return strip

    def across(strip, which, back):
        k, far = (BPT - 1, 0) if back else (0, per_set - 1)
        shift = span if back else width - span
        beyond = which - 1 if back else which + 1
        rolled = pltpu.roll(strip[which][k], shift, 1)
        outside = pltpu.roll(strip[beyond][k], shift, 1) if 0 <= beyond < sets else 0.0
        return jnp.where(group_of == far, outside, rolled)

    def strip_pass(strip, side):
        new = []
        for which in range(sets):
            new.append([])
            for k in range(BPT):
                cell = strip[which][k]
                up = strip[which][k + 1] if k < BPT - 1 else across(strip, which, False)
                down = strip[which][k - 1] if k > 0 else across(strip, which, True)
                around = up + down + pltpu.roll(cell, width - 1, 1) + pltpu.roll(cell, 1, 1)
                new[which].append(cell + strip_coef[side, which, k] * (around - 4.0 * cell))
        return new

    left, right = strip_of(ev - 1, ev), strip_of(ev, ev + 1)
    for repeat in range(PASSES):
        for which in range(sets):
            for k in range(BPT):
                ends[repeat, which, k] = jnp.where(
                    spot == 0,
                    pltpu.roll(left[which][k], width - PASSES + 1, 1),
                    pltpu.roll(right[which][k], width - PASSES - 1, 1),
                )
        if repeat < PASSES - 1:
            left, right = strip_pass(left, 0), strip_pass(right, 1)

    at_end = (lane == width - 1)[None]
    at_start = (lane == 0)[None]

    def diffuse(repeat, field, new_field):
        def chunk(stripe, carry):
            start = stripe * BPT
            main_rows = field[pl.ds(start, BPT + 2)]
            main = main_rows[1:-1]
            shift = lax.rem(width - lax.rem(stripe, per_set) * span, width)
            outside = pltpu.roll(ends[repeat, stripe // per_set], shift, 2)
            around = (
                main_rows[2:] + main_rows[:-2]
                + jnp.where(at_end, outside, pltpu.roll(main, width - 1, 2))
                + jnp.where(at_start, outside, pltpu.roll(main, 1, 2))
            )
            new = main + coef[pl.ds(start, BPT)] * (around - 4.0 * main)
            if new_field is None:
                out[pl.ds(start, BPT)] = new
            else:
                new_field[pl.ds(start + 1, BPT)] = new
            return carry

        return chunk

    now, later = here, there
    for repeat in range(PASSES):
        last = repeat == PASSES - 1
        lax.fori_loop(0, n_sp, diffuse(repeat, now, None if last else later), 0, unroll=4)
        now, later = later, now

    taken(label_span, label_send_sem, label_recv_sem, 1).wait_send()
    for step in range(1, n_ev):
        label_passed(step).wait_send()
    taken(arrived.at[pl.ds(0, n_sp * n_ev - 1)], send_sem, recv_sem.at[0], 1).wait_send()


def solution(mesh):
    n_ev, n_sp = mesh.shape["ev"], mesh.shape["sp"]
    groups = 4

    def per_device(partial_kernels, block_ids, radial_smoother, shell_level, lateral_scale):
        listed, width = partial_kernels.shape[2:]
        shells = shell_level.shape[0]
        rows = lateral_scale.shape[0]
        sets = n_sp // (width // (2 * PASSES))
        field = pltpu.VMEM((rows + 2, shells, width), jnp.float32)
        inner = pltpu.VMEM((rows, shells, width), jnp.float32)
        given = (block_ids, shell_level, partial_kernels, radial_smoother, lateral_scale)
        dma = pltpu.SemaphoreType.DMA
        out = pl.pallas_call(
            functools.partial(kernel, n_ev, n_sp),
            out_shape=jax.ShapeDtypeStruct((rows, shells, width), jnp.float32),
            in_specs=[pl.BlockSpec(memory_space=pltpu.HBM)] * 5,
            out_specs=pl.BlockSpec(memory_space=pltpu.VMEM),
            scratch_shapes=[
                pltpu.SMEM(block_ids.shape, jnp.int32),
                pltpu.SMEM(shell_level.shape, jnp.int32),
                pltpu.VMEM(partial_kernels.shape, jnp.float32),
                pltpu.VMEM(radial_smoother.shape, jnp.float32),
                pltpu.VMEM(lateral_scale.shape, jnp.float32),
                pltpu.VMEM((n_sp, listed * shells, width), jnp.float32),
                pltpu.VMEM((listed, width), jnp.int32),
                pltpu.VMEM((n_sp * n_ev, listed * shells, width), jnp.float32),
                pltpu.VMEM((n_ev, n_sp, listed, width), jnp.int32),
                field, field, inner,
                pltpu.VMEM((2, sets, BPT, shells, width), jnp.float32),
                pltpu.VMEM((sets, n_ev * listed, shells, width), jnp.float32),
                pltpu.VMEM((sets, n_ev * listed, shells, width), jnp.int32),
                pltpu.VMEM((PASSES, sets, BPT, shells, width), jnp.float32),
                dma((5,)), dma, dma((n_sp // groups,)), dma, dma, dma((n_ev,)), dma((n_ev,)),
            ],
            compiler_params=pltpu.CompilerParams(
                collective_id=0, has_side_effects=True, vmem_limit_bytes=40 * 1024 * 1024
            ),
        )(*[pltpu.with_memory_space_constraint(x, pltpu.HBM) for x in given])
        return jnp.transpose(out, (1, 0, 2))

    placed = (P("ev", None, "sp", None), P("ev", "sp"), P(), P("sp"), P())
    return jax.shard_map(
        per_device, mesh=mesh, in_specs=placed, out_specs=P("sp", None, "ev"), check_vma=False
    )
```

```python
import functools

import jax
import jax.numpy as jnp
from jax import lax
from jax.experimental import pallas as pl
from jax.experimental.pallas import tpu as pltpu
from jax.sharding import PartitionSpec as P

BPT = 8
PASSES = 4
NSEG = 4
MESH = pl.DeviceIdType.MESH

diffusion_rate = 0.0615


def halves(value):
    high = value.astype(jnp.bfloat16)
    return high, (value - high.astype(jnp.float32)).astype(jnp.bfloat16)


def product(left, right):
    left_high, left_low = halves(left)
    right_high, right_low = halves(right)
    dot = functools.partial(jnp.dot, preferred_element_type=jnp.float32)
    return dot(left_high, right_high) + (dot(left_high, right_low) + dot(left_low, right_high))


def kernel(
    n_ev, n_sp, ids_in, levels_in, blocks_in, smoother_in, scale_in, out,
    ids, levels, blocks, smoother, scale,
    outgoing, label_out, arrived, labels, here, there, coef, strip_coef, edges, edge_labels, ends,
    load_sem, send_sem, recv_sem, label_send_sem, label_recv_sem,
    label_pass_send_sem, label_pass_recv_sem,
):
    ev, sp = lax.axis_index("ev"), lax.axis_index("sp")
    rows, shells, width = coef.shape
    listed = blocks.shape[2]
    groups = recv_sem.shape[0]
    sets = edges.shape[0]
    span = 2 * PASSES
    per_set = width // span
    size = n_sp // groups

    loads = [
        pltpu.make_async_copy(given, held, load_sem.at[i])
        for i, (given, held) in enumerate(
            [(ids_in, ids), (blocks_in, blocks), (smoother_in, smoother), (levels_in, levels), (scale_in, scale)]
        )
    ]
    for load in loads:
        load.start()

    def holder(step):
        return lax.rem(sp + step, n_sp)

    def peer(step):
        return lax.rem(ev + step, n_ev)

    barrier = pltpu.get_barrier_semaphore()

    def greet(turn, step, carry):
        pl.semaphore_signal(barrier, inc=1, device_id=(peer(turn), holder(step)), device_id_type=MESH)
        return carry

    for turn in range(n_ev):
        lax.fori_loop(int(turn == 0), n_sp, functools.partial(greet, turn), 0)

    for load in loads[:3]:
        load.wait()
    columns = []
    for j in range(listed):
        block_id = ids[0, j]
        label_out[j : j + 1, :] = jnp.full((1, width), block_id // NSEG, jnp.int32)
        segment = lax.rem(block_id, NSEG)
        block = blocks[0, :, j, :]
        columns.append(
            jnp.concatenate([block * (segment == q).astype(jnp.float32) for q in range(NSEG)], axis=0)
        )
    smooth = product(smoother[...], jnp.concatenate(columns, axis=1))
    for m in range(n_sp):
        for j in range(listed):
            outgoing[m, j * shells : (j + 1) * shells, :] = smooth[
                m * shells : (m + 1) * shells, j * width : (j + 1) * width
            ]

    pl.semaphore_wait(barrier, n_sp * n_ev - 1)

    def label_copy(step):
        return pltpu.make_async_remote_copy(
            src_ref=label_out, dst_ref=labels.at[0, step], send_sem=label_send_sem,
            recv_sem=label_recv_sem, device_id=(ev, holder(step)), device_id_type=MESH,
        )

    def copy(step, turn):
        return pltpu.make_async_remote_copy(
            src_ref=outgoing.at[holder(step)], dst_ref=arrived.at[step * n_ev + turn], send_sem=send_sem,
            recv_sem=recv_sem.at[step // size], device_id=(peer(turn), holder(step)), device_id_type=MESH,
        )

    def send_label(step, carry):
        label_copy(step).start()
        return carry

    def send(step, carry):
        for turn in range(n_ev):
            copy(step, turn).start()
        return carry

    for turn in range(1, n_ev):
        copy(0, turn).start()
    lax.fori_loop(1, size, send, 0)
    lax.fori_loop(1, n_sp, send_label, 0)
    lax.fori_loop(size, n_sp, send, 0)

    arrived[0] = outgoing[sp]
    labels[0, 0] = label_out[...]

    for load in loads[3:]:
        load.wait()
    shell_of = lax.broadcasted_iota(jnp.int32, (shells, width), 0)
    level = jnp.zeros((shells, width), jnp.float32)
    for r in range(shells):
        level = jnp.where(shell_of == r, levels[r].astype(jnp.float32), level)
    level = diffusion_rate * level
    lane = lax.broadcasted_iota(jnp.int32, (1, width), 1)
    spot = lane & (span - 1)
    group_of = lax.shift_right_logical(lane, span.bit_length() - 1)
    late_half = lane >= width // 2
    after = jnp.minimum(ev + 1, n_ev - 1)
    before = jnp.maximum(ev - 1, 0)
    has_after = (ev + 1 < n_ev).astype(jnp.float32)
    has_before = (ev > 0).astype(jnp.float32)

    def tile(start, which):
        return scale[pl.ds(start, BPT), pl.ds(pl.multiple_of(which * width, width), width)]

    left_scale = [jnp.zeros((BPT, width), jnp.float32)] * sets
    right_scale = list(left_scale)
    for stripe in range(n_sp):
        start = stripe * BPT
        main = tile(start, ev)
        coef[pl.ds(start, BPT)] = level[None] * main[:, None, :]
        which, local = divmod(stripe, per_set)
        shift = (local * span + PASSES) % width
        left = jnp.where(late_half, tile(start, before) * has_before, main)
        right = jnp.where(late_half, main, tile(start, after) * has_after)
        mine = group_of == local
        left_scale[which] = jnp.where(mine, pltpu.roll(left, shift, 1), left_scale[which])
        right_scale[which] = jnp.where(mine, pltpu.roll(right, shift, 1), right_scale[which])
    for which in range(sets):
        strip_coef[0, which] = level[None] * left_scale[which][:, None, :]
        strip_coef[1, which] = level[None] * right_scale[which][:, None, :]
        for entry in range(n_ev * listed):
            edges[which, entry] = jnp.zeros((shells, width), jnp.float32)
            edge_labels[which, entry] = jnp.full((shells, width), -n_ev * n_sp * BPT * span, jnp.int32)

    blank = jnp.zeros((1, shells, width), jnp.float32)
    for field in (here, there):
        field[0:1] = blank
        field[rows + 1 : rows + 2] = blank

    def taken(buffer, one, two, step):
        return pltpu.make_async_remote_copy(
            src_ref=buffer, dst_ref=buffer, send_sem=one, recv_sem=two,
            device_id=(peer(step), sp), device_id_type=MESH,
        )

    def label_passed(step):
        return pltpu.make_async_remote_copy(
            src_ref=labels.at[0], dst_ref=labels.at[step],
            send_sem=label_pass_send_sem.at[step], recv_sem=label_pass_recv_sem.at[step],
            device_id=(peer(step), sp), device_id_type=MESH,
        )

    def place(slot, carry):
        stripe = lax.rem(sp - slot + n_sp, n_sp)
        start = stripe * BPT + 1
        which, local = stripe // per_set, lax.rem(stripe, per_set)
        shift = lax.rem(local * span + PASSES, width)
        mine = group_of == local
        main = [jnp.zeros((shells, width), jnp.float32) for _ in range(BPT)]
        for turn in range(n_ev):
            for j in range(listed):
                block = arrived[slot * n_ev + turn, j * shells : (j + 1) * shells, :]
                label = jnp.broadcast_to(labels[turn, slot, j : j + 1, :], (shells, width))
                entry = turn * listed + j
                edges[which, entry] = jnp.where(mine, pltpu.roll(block, shift, 1), edges[which, entry])
                edge_labels[which, entry] = jnp.where(mine, label, edge_labels[which, entry])
                in_main = label - ev * BPT
                for k in range(BPT):
                    main[k] = main[k] + jnp.where(in_main == k, block, 0.0)
        for k in range(BPT):
            here[start + k] = main[k]
        return carry

    label_span = labels.at[0, pl.ds(0, n_sp - 1)]
    taken(label_span, label_send_sem, label_recv_sem, 1).wait_recv()
    for step in range(1, n_ev):
        label_passed(step).start()
    for group in range(groups):
        count = size * n_ev - (group == 0)
        taken(arrived.at[pl.ds(0, count)], send_sem, recv_sem.at[group], 1).wait_recv()
        if group == 0:
            for step in range(1, n_ev):
                label_passed(step).wait_recv()
        lax.fori_loop(group * size, (group + 1) * size, place, 0, unroll=2)

    def strip_of(inner, outer):
        base = jnp.where(spot < PASSES, inner, outer) * BPT
        strip = []
        for which in range(sets):
            found = [edge_labels[which, entry] - base for entry in range(n_ev * listed)]
            values = [edges[which, entry] for entry in range(n_ev * listed)]
            strip.append([
                sum(jnp.where(at == k, value, 0.0) for at, value in zip(found, values)) for k in range(BPT)
            ])
        return strip

    def across(strip, which, back):
        k, far = (BPT - 1, 0) if back else (0, per_set - 1)
        shift = span if back else width - span
        beyond = which - 1 if back else which + 1
        rolled = pltpu.roll(strip[which][k], shift, 1)
        outside = pltpu.roll(strip[beyond][k], shift, 1) if 0 <= beyond < sets else 0.0
        return jnp.where(group_of == far, outside, rolled)

    def strip_pass(strip, side):
        new = []
        for which in range(sets):
            new.append([])
            for k in range(BPT):
                cell = strip[which][k]
                up = strip[which][k + 1] if k < BPT - 1 else across(strip, which, False)
                down = strip[which][k - 1] if k > 0 else across(strip, which, True)
                around = up + down + pltpu.roll(cell, width - 1, 1) + pltpu.roll(cell, 1, 1)
                new[which].append(cell + strip_coef[side, which, k] * (around - 4.0 * cell))
        return new

    left, right = strip_of(ev - 1, ev), strip_of(ev, ev + 1)
    at_end = (lane == width - 1)[None]
    at_start = (lane == 0)[None]

    def diffuse(repeat, field, new_field):
        def chunk(stripe, carry):
            start = stripe * BPT
            main_rows = field[pl.ds(start, BPT + 2)]
            main = main_rows[1:-1]
            shift = (width - stripe % per_set * span) % width
            outside = pltpu.roll(ends[repeat, stripe // per_set], shift, 2)
            around = (
                main_rows[2:] + main_rows[:-2]
                + jnp.where(at_end, outside, pltpu.roll(main, width - 1, 2))
                + jnp.where(at_start, outside, pltpu.roll(main, 1, 2))
            )
            new = main + coef[pl.ds(start, BPT)] * (around - 4.0 * main)
            if new_field is None:
                out[pl.ds(start, BPT)] = new
            else:
                new_field[pl.ds(start + 1, BPT)] = new
            return carry

        return chunk

    now, later = here, there
    for repeat in range(PASSES):
        last = repeat == PASSES - 1
        for which in range(sets):
            for k in range(BPT):
                ends[repeat, which, k] = jnp.where(
                    spot == 0,
                    pltpu.roll(left[which][k], width - PASSES + 1, 1),
                    pltpu.roll(right[which][k], width - PASSES - 1, 1),
                )
        if not last:
            left, right = strip_pass(left, 0), strip_pass(right, 1)
        chunk = diffuse(repeat, now, None if last else later)
        if n_sp <= 16:
            for stripe in range(n_sp):
                chunk(stripe, 0)
        else:
            lax.fori_loop(0, n_sp, chunk, 0, unroll=4)
        now, later = later, now

    taken(label_span, label_send_sem, label_recv_sem, 1).wait_send()
    for step in range(1, n_ev):
        label_passed(step).wait_send()
    taken(arrived.at[pl.ds(0, n_sp * n_ev - 1)], send_sem, recv_sem.at[0], 1).wait_send()


def solution(mesh):
    n_ev, n_sp = mesh.shape["ev"], mesh.shape["sp"]
    groups = 4

    def per_device(partial_kernels, block_ids, radial_smoother, shell_level, lateral_scale):
        listed, width = partial_kernels.shape[2:]
        shells = shell_level.shape[0]
        rows = lateral_scale.shape[0]
        sets = n_sp // (width // (2 * PASSES))
        field = pltpu.VMEM((rows + 2, shells, width), jnp.float32)
        inner = pltpu.VMEM((rows, shells, width), jnp.float32)
        given = (block_ids, shell_level, partial_kernels, radial_smoother, lateral_scale)
        dma = pltpu.SemaphoreType.DMA
        out = pl.pallas_call(
            functools.partial(kernel, n_ev, n_sp),
            out_shape=jax.ShapeDtypeStruct((rows, shells, width), jnp.float32),
            in_specs=[pl.BlockSpec(memory_space=pltpu.HBM)] * 5,
            out_specs=pl.BlockSpec(memory_space=pltpu.VMEM),
            scratch_shapes=[
                pltpu.SMEM(block_ids.shape, jnp.int32),
                pltpu.SMEM(shell_level.shape, jnp.int32),
                pltpu.VMEM(partial_kernels.shape, jnp.float32),
                pltpu.VMEM(radial_smoother.shape, jnp.float32),
                pltpu.VMEM(lateral_scale.shape, jnp.float32),
                pltpu.VMEM((n_sp, listed * shells, width), jnp.float32),
                pltpu.VMEM((listed, width), jnp.int32),
                pltpu.VMEM((n_sp * n_ev, listed * shells, width), jnp.float32),
                pltpu.VMEM((n_ev, n_sp, listed, width), jnp.int32),
                field, field, inner,
                pltpu.VMEM((2, sets, BPT, shells, width), jnp.float32),
                pltpu.VMEM((sets, n_ev * listed, shells, width), jnp.float32),
                pltpu.VMEM((sets, n_ev * listed, shells, width), jnp.int32),
                pltpu.VMEM((PASSES, sets, BPT, shells, width), jnp.float32),
                dma((5,)), dma, dma((groups,)), dma, dma, dma((n_ev,)), dma((n_ev,)),
            ],
            compiler_params=pltpu.CompilerParams(
                collective_id=0, has_side_effects=True, vmem_limit_bytes=40 * 1024 * 1024
            ),
        )(*[pltpu.with_memory_space_constraint(x, pltpu.HBM) for x in given])
        return jnp.transpose(out, (1, 0, 2))

    placed = (P("ev", None, "sp", None), P("ev", "sp"), P(), P("sp"), P())
    return jax.shard_map(
        per_device, mesh=mesh, in_specs=placed, out_specs=P("sp", None, "ev"), check_vma=False
    )
```
